32 devices in a mesh: batch: 4 (over y, x), head: 8 (over z, core).
Axes of the slice: x: 2, y: 2, z: 4, core: 2. Of those that a mesh axis runs over, the one named last changes fastest.
Arguments:
- layer_source: bfloat16 [16384, 2048], P(('batch', 'head')), may hold values from -6 to 6
- piecewise_opening_memory: float32 [4, 32, 64, 64], P('batch', 'head'), may hold values from -18 to 18
- upstream_adjoint: bfloat16 [16384, 2048], P(('batch', 'head')), may hold values from -6 to 6
- earlier_layernorm_scale: float32 [2048], replicated, may hold values from 0.25 to 1.75
- earlier_layernorm_shift: float32 [2048], replicated, may hold values from -1.8 to 1.8
- accept_blend: float32 [2048], replicated, may hold values from 0 to 1
- lookup_blend: float32 [2048], replicated, may hold values from 0 to 1
- payload_blend: float32 [2048], replicated, may hold values from 0 to 1
- valve_blend: float32 [2048], replicated, may hold values from 0 to 1
- accept_weights: bfloat16 [2048, 2048], P('batch', 'head'), may hold values from -0.125 to 0.125
- lookup_weights: bfloat16 [2048, 2048], P('batch', 'head'), may hold values from -0.125 to 0.125
- payload_weights: bfloat16 [2048, 2048], P('batch', 'head'), may hold values from -0.125 to 0.125
- valve_weights: bfloat16 [2048, 2048], P('batch', 'head'), may hold values from -0.125 to 0.125
- forgetting_loglog: float32 [32, 64], P('head'), may hold values from -8 to -3.4
- diagonal_boost: float32 [32, 64], P('head'), may hold values from 0 to 1.5
- groupwise_scale: float32 [2048], P('head'), may hold values from 0.25 to 1.75
- groupwise_shift: float32 [2048], P('head'), may hold values from -1.8 to 1.8
- emission_weights: bfloat16 [2048, 2048], P('head', 'batch'), may hold values from -0.25 to 0.25
- later_layernorm_scale: float32 [2048], replicated, may hold values from 0.25 to 1.75
- later_layernorm_shift: float32 [2048], replicated, may hold values from -1.8 to 1.8
- feedforward_lookup_blend: float32 [2048], replicated, may hold values from 0 to 1
- feedforward_accept_blend: float32 [2048], replicated, may hold values from 0 to 1
- feedforward_lookup_weights: bfloat16 [2048, 7168], P('batch', 'head'), may hold values from -0.125 to 0.125
- feedforward_payload_weights: bfloat16 [7168, 2048], P('head', 'batch'), may hold values from -0.0625 to 0.0625
- feedforward_accept_weights: bfloat16 [2048, 2048], P('batch', 'head'), may hold values from -0.125 to 0.125
Outputs:
- block_out: bfloat16 [16384, 2048], P(('batch', 'head'))
- in_grad: float32 [16384, 2048], P(('batch', 'head'))
- initial_state_gradient: float32 [4, 32, 64, 64], P('batch', 'head')
- ln1_gain_grad: float32 [2048], replicated
- ln1_bias_grad: float32 [2048], replicated
- mix_r_grad: float32 [2048], replicated
- mix_k_grad: float32 [2048], replicated
- mix_v_grad: float32 [2048], replicated
- mix_g_grad: float32 [2048], replicated
- weight_r_grad: float32 [2048, 2048], P('batch', 'head')
- weight_k_grad: float32 [2048, 2048], P('batch', 'head')
- weight_v_grad: float32 [2048, 2048], P('batch', 'head')
- weight_g_grad: float32 [2048, 2048], P('batch', 'head')
- decay_grad: float32 [32, 64], P('head')
- diagonal_boost_deriv: float32 [32, 64], P('head')
- group_gain_grad: float32 [2048], P('head')
- group_bias_grad: float32 [2048], P('head')
- weight_o_grad: float32 [2048, 2048], P('head', 'batch')
- ln2_gain_grad: float32 [2048], replicated
- ln2_bias_grad: float32 [2048], replicated
- chan_mix_k_grad: float32 [2048], replicated
- chan_mix_r_grad: float32 [2048], replicated
- chan_key_grad: float32 [2048, 7168], P('batch', 'head')
- chan_value_grad: float32 [7168, 2048], P('head', 'batch')
- chan_recept_grad: float32 [2048, 2048], P('batch', 'head')
The draws below stay inside these ranges and needn't reach their ends.
All inputs are finite; a program needn't handle non-finite values.
Results may differ from the reference program's by a relative error of at most 0.03.
Values may be sent and summed in bfloat16 or wider, within the bound.
A program may use at most 512 MiB of HBM per device.

```python
import jax
import jax.numpy as jnp
from jax import lax

D = 2048
ATTN_NUMBER = 32
FF = 7168
SEG_LEN = 4096
ATTN_WIDTH = 64
SEGS = 4
TOKENS = 16384


def levels(own_key, shape, split, least, top_value):
    loudness = 1.0
    for position, shards_of in split:
        heights = jax.random.uniform(jax.random.fold_in(jax.random.fold_in(own_key, 6), position), (shards_of,), jnp.float32, least / len(split), top_value / len(split))
        loudness = loudness * jnp.repeat(jnp.exp(heights), shape[position] // shards_of).reshape((-1,) + (1,) * (len(shape) - 1 - position))
    return loudness


def gaussian(rng, extent, width, reach, shards=(), dtype=jnp.bfloat16):
    drawn = jax.random.normal(rng, extent, jnp.float32) * width
    if len(shards) > 0:
        drawn = levels(rng, extent, shards, -0.22, 0.18) * drawn
    return jnp.clip(drawn, min=-reach, max=reach).astype(dtype)


def setup_inputs(seed: int = 0) -> dict:
    key_of = jax.random.split(jax.random.key(seed), 26)
    layer_source = gaussian(key_of[0], (TOKENS, D), 1.0, 6.0, ((0, 32),))
    piecewise_opening_memory = gaussian(key_of[1], (SEGS, ATTN_NUMBER, ATTN_WIDTH, ATTN_WIDTH), 3.0, 18.0, ((0, 4), (1, 8)), jnp.float32)
    upstream_adjoint = gaussian(key_of[2], (TOKENS, D), 1.0, 6.0, ((0, 32),))
    earlier_layernorm_scale = jnp.clip(1.0 + 0.15 * jax.random.normal(key_of[3], (D,), jnp.float32), 0.25, 1.75)
    earlier_layernorm_shift = gaussian(key_of[4], (D,), 0.3, 1.8, (), jnp.float32)
    accept_blend = jnp.clip(jax.random.uniform(key_of[5], (D,), jnp.float32, 0.0, 1.0), 0.0, 1.0)
    lookup_blend = jnp.clip(jax.random.uniform(key_of[6], (D,), jnp.float32, 0.0, 1.0), 0.0, 1.0)
    payload_blend = jnp.clip(jax.random.uniform(key_of[7], (D,), jnp.float32, 0.0, 1.0), 0.0, 1.0)
    valve_blend = jnp.clip(jax.random.uniform(key_of[8], (D,), jnp.float32, 0.0, 1.0), 0.0, 1.0)
    accept_weights = gaussian(key_of[9], (D, D), D ** -0.5, 0.125, ((0, 4), (1, 8)))
    lookup_weights = gaussian(key_of[10], (D, D), D ** -0.5, 0.125, ((0, 4), (1, 8)))
    payload_weights = gaussian(key_of[11], (D, D), D ** -0.5, 0.125, ((0, 4), (1, 8)))
    valve_weights = gaussian(key_of[12], (D, D), D ** -0.5, 0.125, ((0, 4), (1, 8)))
    forgetting_loglog = jnp.clip(-8.0 + 4.6 * jax.random.uniform(key_of[13], (ATTN_NUMBER, ATTN_WIDTH), jnp.float32) ** levels(key_of[13], (ATTN_NUMBER, ATTN_WIDTH), ((0, 8),), -0.2, 0.2), -8.0, -3.4)
    diagonal_boost = jnp.clip(1.5 * jax.random.uniform(key_of[14], (ATTN_NUMBER, ATTN_WIDTH), jnp.float32) ** levels(key_of[14], (ATTN_NUMBER, ATTN_WIDTH), ((0, 8),), -0.2, 0.2), 0.0, 1.5)
    groupwise_scale = jnp.clip(1.0 + 0.15 * jax.random.normal(key_of[15], (D,), jnp.float32), 0.25, 1.75)
    groupwise_shift = gaussian(key_of[16], (D,), 0.3, 1.8, ((0, 8),), jnp.float32)
    emission_weights = gaussian(key_of[17], (D, D), (D // 4) ** -0.5, 0.25, ((0, 8), (1, 4)))
    later_layernorm_scale = jnp.clip(1.0 + 0.15 * jax.random.normal(key_of[18], (D,), jnp.float32), 0.25, 1.75)
    later_layernorm_shift = gaussian(key_of[19], (D,), 0.3, 1.8, (), jnp.float32)
    feedforward_lookup_blend = jnp.clip(jax.random.uniform(key_of[20], (D,), jnp.float32, 0.0, 1.0), 0.0, 1.0)
    feedforward_accept_blend = jnp.clip(jax.random.uniform(key_of[21], (D,), jnp.float32, 0.0, 1.0), 0.0, 1.0)
    feedforward_lookup_weights = gaussian(key_of[22], (D, FF), D ** -0.5, 0.125, ((0, 4), (1, 8)))
    feedforward_payload_weights = gaussian(key_of[23], (FF, D), FF ** -0.5, 0.0625, ((0, 8), (1, 4)))
    feedforward_accept_weights = gaussian(key_of[24], (D, D), D ** -0.5, 0.125, ((0, 4), (1, 8)))
    return {"layer_source": layer_source, "piecewise_opening_memory": piecewise_opening_memory, "upstream_adjoint": upstream_adjoint, "earlier_layernorm_scale": earlier_layernorm_scale, "earlier_layernorm_shift": earlier_layernorm_shift, "accept_blend": accept_blend, "lookup_blend": lookup_blend, "payload_blend": payload_blend, "valve_blend": valve_blend, "accept_weights": accept_weights, "lookup_weights": lookup_weights, "payload_weights": payload_weights, "valve_weights": valve_weights, "forgetting_loglog": forgetting_loglog, "diagonal_boost": diagonal_boost, "groupwise_scale": groupwise_scale, "groupwise_shift": groupwise_shift, "emission_weights": emission_weights, "later_layernorm_scale": later_layernorm_scale, "later_layernorm_shift": later_layernorm_shift, "feedforward_lookup_blend": feedforward_lookup_blend, "feedforward_accept_blend": feedforward_accept_blend, "feedforward_lookup_weights": feedforward_lookup_weights, "feedforward_payload_weights": feedforward_payload_weights, "feedforward_accept_weights": feedforward_accept_weights}


ln_eps = 1e-05
gn_eps = 0.00064
highest = lax.Precision.HIGHEST

@jax.custom_vjp
def low(v):
    return lax.optimization_barrier(v.astype(jnp.bfloat16)).astype(jnp.float32)

@jax.custom_vjp
def low_back(v):
    return v

def low_keep(v):
    return (low(v), None)

def low_pass(kept, grad):
    return (grad,)

def back_keep(v):
    return (v, None)

def back_low(kept, grad):
    return (low(grad),)
low.defvjp(low_keep, low_pass)
low_back.defvjp(back_keep, back_low)

def matmul_high(left, right):
    return jnp.dot(left, right, precision=highest, preferred_element_type=jnp.float32)

def layer_norm(payload_lines, gain, bias):
    center = payload_lines - lax.optimization_barrier(jnp.mean(payload_lines, -1, keepdims=True))
    return center * lax.rsqrt(lax.optimization_barrier(jnp.mean(center * center, -1, keepdims=True)) + ln_eps) * gain + bias

def shift_down(payload_lines):
    return jnp.concatenate([jnp.zeros_like(payload_lines[:1]), payload_lines[:-1]], 0)

def token_mix(current, earlier, weight):
    return low(current * weight + earlier * (1.0 - weight))

def rounded_both(payload_lines):
    return low(low_back(payload_lines))

def loop_update(accept_lines, lookup_lines, payload_lines, forgetting_loglog, diagonal_boost, attn_memory):
    length = accept_lines.shape[0]
    block_len = 64
    keep = jnp.exp(-jnp.exp(forgetting_loglog))

    def block_list(tensor_entry):
        return tensor_entry.reshape(length // block_len, block_len, ATTN_NUMBER, ATTN_WIDTH)

    def token_step(carried_memory, inputs):
        present_accept, keys_now, values_now = inputs
        tensor_dyad = keys_now[:, :, None] * values_now[:, None, :]
        ultimate_answer = lax.optimization_barrier(jnp.sum(present_accept[:, :, None] * (carried_memory + diagonal_boost[:, :, None] * tensor_dyad), axis=1))
        return (keep[:, :, None] * carried_memory + tensor_dyad, ultimate_answer)

    @jax.checkpoint
    def block_step(carried_memory, inputs):
        return lax.scan(token_step, carried_memory, inputs)
    final_state, outputs = lax.scan(block_step, attn_memory, (block_list(accept_lines), block_list(lookup_lines), block_list(payload_lines)))
    return outputs.reshape(length, D)

def forward(learnable_tensors, layer_source, attn_memory):
    earlier_layernorm_scale, earlier_layernorm_shift, accept_blend, lookup_blend, payload_blend, valve_blend, accept_weights, lookup_weights, payload_weights, valve_weights, forgetting_loglog, diagonal_boost, groupwise_scale, groupwise_shift, emission_weights, later_layernorm_scale, later_layernorm_shift, feedforward_lookup_blend, feedforward_accept_blend, feedforward_lookup_weights, feedforward_payload_weights, feedforward_accept_weights = learnable_tensors
    normed1 = low(layer_norm(layer_source, earlier_layernorm_scale, earlier_layernorm_shift))
    prev1 = shift_down(normed1)
    accept_lines = rounded_both(matmul_high(token_mix(normed1, prev1, accept_blend), accept_weights))
    lookup_lines = rounded_both(matmul_high(token_mix(normed1, prev1, lookup_blend), lookup_weights))
    payload_lines = rounded_both(matmul_high(token_mix(normed1, prev1, payload_blend), payload_weights))
    gate = jax.nn.silu(low_back(matmul_high(token_mix(normed1, prev1, valve_blend), valve_weights)))
    blended_source = loop_update(accept_lines, lookup_lines, payload_lines, forgetting_loglog, diagonal_boost, attn_memory)
    heads = blended_source.reshape(-1, ATTN_NUMBER, ATTN_WIDTH)
    center = heads - lax.optimization_barrier(jnp.mean(heads, -1, keepdims=True))
    normed_heads = center * lax.rsqrt(lax.optimization_barrier(jnp.mean(center * center, -1, keepdims=True)) + gn_eps)
    grouped = normed_heads.reshape(-1, D) * groupwise_scale + groupwise_shift
    mixer = low_back(matmul_high(low(grouped * gate), emission_weights))
    middle = layer_source + mixer
    normed2 = low(layer_norm(middle, later_layernorm_scale, later_layernorm_shift))
    prev2 = shift_down(normed2)
    key_pre = low_back(matmul_high(token_mix(normed2, prev2, feedforward_lookup_blend), feedforward_lookup_weights))
    key_sq = low(jnp.square(jax.nn.relu(key_pre)))
    value_sum = low_back(matmul_high(key_sq, feedforward_payload_weights))
    recept2 = low_back(matmul_high(token_mix(normed2, prev2, feedforward_accept_blend), feedforward_accept_weights))
    return middle + jax.nn.sigmoid(recept2) * value_sum

def reference(layer_source, piecewise_opening_memory, upstream_adjoint, earlier_layernorm_scale, earlier_layernorm_shift, accept_blend, lookup_blend, payload_blend, valve_blend, accept_weights, lookup_weights, payload_weights, valve_weights, forgetting_loglog, diagonal_boost, groupwise_scale, groupwise_shift, emission_weights, later_layernorm_scale, later_layernorm_shift, feedforward_lookup_blend, feedforward_accept_blend, feedforward_lookup_weights, feedforward_payload_weights, feedforward_accept_weights):
    learnable_tensors = tuple((tensor_entry.astype(jnp.float32) for tensor_entry in (earlier_layernorm_scale, earlier_layernorm_shift, accept_blend, lookup_blend, payload_blend, valve_blend, accept_weights, lookup_weights, payload_weights, valve_weights, forgetting_loglog, diagonal_boost, groupwise_scale, groupwise_shift, emission_weights, later_layernorm_scale, later_layernorm_shift, feedforward_lookup_blend, feedforward_accept_blend, feedforward_lookup_weights, feedforward_payload_weights, feedforward_accept_weights)))
    inputs = layer_source.astype(jnp.float32).reshape(SEGS, SEG_LEN, D)
    cotangents = upstream_adjoint.astype(jnp.float32).reshape(SEGS, SEG_LEN, D)

    def one_segment(totals, pieces):
        seg_in, seg_state, seg_cot = pieces
        seg_out, pullback = jax.vjp(forward, learnable_tensors, seg_in, seg_state)
        grad_params, grad_in, grad_state = pullback(seg_cot)
        totals = jax.tree.map(lambda left, right: left + right, totals, grad_params)
        return (totals, (seg_out, grad_in, grad_state))
    zeros = jax.tree.map(jnp.zeros_like, learnable_tensors)
    totals, stacked = lax.scan(one_segment, zeros, (inputs, piecewise_opening_memory.astype(jnp.float32), cotangents))
    seg_outs, in_grads, state_grads = stacked
    block_out = seg_outs.reshape(TOKENS, D).astype(jnp.bfloat16)
    in_grad = in_grads.reshape(TOKENS, D)
    return (block_out, in_grad, state_grads, totals[0], totals[1], totals[2], totals[3], totals[4], totals[5], totals[6], totals[7], totals[8], totals[9], totals[10], totals[11], totals[12], totals[13], totals[14], totals[15], totals[16], totals[17], totals[18], totals[19], totals[20], totals[21])
```

```python
import functools

import jax
import jax.numpy as jnp
from jax import lax
from jax.experimental import pallas as pl
from jax.experimental.pallas import tpu as pltpu
from jax.sharding import Mesh
from jax.sharding import PartitionSpec as P

ATTN_WIDTH = 64
QUAD = 256

ln_eps = 1e-05
gn_eps = 0.00064
f32 = jnp.float32
bf16 = jnp.bfloat16


def nn(left, right):
    return jnp.dot(left, right, preferred_element_type=f32)


def nt(left, right):
    return lax.dot_general(left, right, (((1,), (1,)), ((), ())), preferred_element_type=f32)


def tn(left, right):
    return lax.dot_general(left, right, (((0,), (0,)), ((), ())), preferred_element_type=f32)


def head_masks():
    lane_head = lax.broadcasted_iota(jnp.int32, (1, QUAD), 1) // ATTN_WIDTH
    return [lane_head == h for h in range(QUAD // ATTN_WIDTH)]


def block_mask():
    row_head = lax.broadcasted_iota(jnp.int32, (QUAD, QUAD), 0) // ATTN_WIDTH
    col_head = lax.broadcasted_iota(jnp.int32, (QUAD, QUAD), 1) // ATTN_WIDTH
    return row_head == col_head


def only(mask, lines):
    return jnp.where(mask, lines, jnp.zeros_like(lines))


def compress(square, masks):
    return sum(
        jnp.where(m, square[h * ATTN_WIDTH : (h + 1) * ATTN_WIDTH, :], 0.0)
        for h, m in enumerate(masks)
    )


def expand(packed, blocks):
    return jnp.where(blocks, jnp.concatenate([packed] * (QUAD // ATTN_WIDTH), 0), 0.0)


def head_sum(lines, ones):
    return nn(lines.astype(bf16), ones)


def head_sum_fine(lines, ones):
    coarse = lines.astype(bf16)
    return nn(coarse, ones) + nn((lines - coarse.astype(f32)).astype(bf16), ones)


def local_state_kernel(rate_ref, k_ref, v_ref, out_ref):
    length = k_ref.shape[1]
    rate = rate_ref[...]
    remaining = (length - 1) - lax.broadcasted_iota(jnp.int32, (length, 1), 0)
    faded = (k_ref[0].astype(f32) * jnp.exp(-rate * remaining.astype(f32))).astype(bf16)
    out_ref[0] = compress(tn(v_ref[0], faded), head_masks())


def group_norm_parts(y, ones):
    center = y - head_sum_fine(y, ones) * (1.0 / ATTN_WIDTH)
    inv = lax.rsqrt(head_sum(center * center, ones) * (1.0 / ATTN_WIDTH) + gn_eps)
    return center * inv, inv


def forward_kernel(
    rate_ref, boost_ref, gain_ref, bias_ref, s0_ref, r_ref, k_ref, v_ref, g_ref,
    z_ref, y_ref, begin_ref, state,
):
    span = r_ref.shape[1]
    masks = head_masks()
    blocks = block_mask()
    ones = jnp.where(blocks, 1.0, 0.0).astype(bf16)

    @pl.when(pl.program_id(2) == 0)
    def _():
        state[...] = expand(s0_ref[0], blocks)

    rate = rate_ref[...]
    pos = lax.broadcasted_iota(jnp.int32, (span, 1), 0).astype(f32)
    r = r_ref[0].astype(f32)
    k = k_ref[0].astype(f32)
    v = v_ref[0]
    qt = (r * jnp.exp(-rate * pos)).astype(bf16)
    kt = (k * jnp.exp(rate * (pos + 1.0))).astype(bf16)
    begin = state[...]
    begin_ref[0, 0] = compress(begin, masks)
    y = nt(qt, begin.astype(bf16))
    causal = lax.broadcasted_iota(jnp.int32, (span, span), 0) > lax.broadcasted_iota(
        jnp.int32, (span, span), 1
    )
    for m in masks:
        scores = jnp.where(causal, nt(only(m, qt), kt), 0.0).astype(bf16)
        y = y + nn(scores, only(m, v))
    y = y + head_sum(r * boost_ref[...] * k, ones) * v.astype(f32)
    state[...] = jnp.exp(-rate * span) * (begin + jnp.where(blocks, tn(v, kt), 0.0))
    y_ref[0] = y
    normed, _ = group_norm_parts(y, ones)
    g = g_ref[0]
    z_ref[0] = ((normed * gain_ref[...] + bias_ref[...]) * (g * jax.nn.sigmoid(g))).astype(bf16)


def gate_back_kernel(
    rate_ref, gain_ref, bias_ref, gz_ref, y_ref, g_ref, r_ref,
    gg_ref, gy_ref, end_ref, sums_ref, total,
):
    span = r_ref.shape[1]
    step = pl.program_id(2)
    blocks = block_mask()
    ones = jnp.where(blocks, 1.0, 0.0).astype(bf16)

    @pl.when(step == 0)
    def _():
        total[...] = jnp.zeros_like(total)
        sums_ref[...] = jnp.zeros_like(sums_ref)

    normed, inv = group_norm_parts(y_ref[0], ones)
    gain = gain_ref[...]
    g = g_ref[0]
    gz = gz_ref[0].astype(f32)
    sig = jax.nn.sigmoid(g)
    grad_grouped = gz * (g * sig)
    grouped = normed * gain + bias_ref[...]
    gg_ref[0] = (gz * grouped * sig * (1.0 + g * (1.0 - sig))).astype(bf16)
    sums_ref[0, 0, 0:1, :] += jnp.sum(grad_grouped * normed, 0, keepdims=True)
    sums_ref[0, 0, 1:2, :] += jnp.sum(grad_grouped, 0, keepdims=True)
    e = grad_grouped * gain
    gy = inv * (
        e
        - head_sum_fine(e, ones) * (1.0 / ATTN_WIDTH)
        - normed * (head_sum(e * normed, ones) * (1.0 / ATTN_WIDTH))
    )
    gy = gy.astype(bf16)
    gy_ref[0] = gy
    pos = (lax.broadcasted_iota(jnp.int32, (span, 1), 0) + step * span).astype(f32)
    faded = (r_ref[0].astype(f32) * jnp.exp(-rate_ref[...] * pos)).astype(bf16)
    total[...] += tn(gy, faded)
    end_ref[0] = compress(total[...], head_masks())


def backward_kernel(
    rate_ref, boost_ref, end_ref, begin_ref, r_ref, k_ref, v_ref, gy_ref,
    dr_ref, dk_ref, dv_ref, sums_ref, carry,
):
    span = r_ref.shape[1]
    masks = head_masks()
    blocks = block_mask()
    ones = jnp.where(blocks, 1.0, 0.0).astype(bf16)

    @pl.when(pl.program_id(2) == 0)
    def _():
        carry[...] = expand(end_ref[0], blocks)
        sums_ref[...] = jnp.zeros_like(sums_ref)

    rate = rate_ref[...]
    boost = boost_ref[...]
    pos = lax.broadcasted_iota(jnp.int32, (span, 1), 0).astype(f32)
    toward = jnp.exp(-rate * pos)
    away = jnp.exp(rate * (pos + 1.0))
    r = r_ref[0].astype(f32)
    k = k_ref[0].astype(f32)
    v = v_ref[0]
    gy = gy_ref[0]
    qt = (r * toward).astype(bf16)
    kt = (k * away).astype(bf16)
    passed = jnp.exp(-rate * span) * carry[...]
    passed_low = passed.astype(bf16)
    begin = expand(begin_ref[0, 0], blocks)
    rows = lax.broadcasted_iota(jnp.int32, (span, span), 0)
    cols = lax.broadcasted_iota(jnp.int32, (span, span), 1)
    dq = nn(gy, begin.astype(bf16))
    dk = nn(v, passed_low)
    dv = nt(kt, passed_low)
    for m in masks:
        v_h, gy_h, k_h, q_h = only(m, v), only(m, gy), only(m, kt), only(m, qt)
        pairs = jnp.where(rows > cols, nt(gy_h, v), 0.0).astype(bf16)
        dq = dq + nn(pairs, k_h)
        pairs_t = jnp.where(rows < cols, nt(v_h, gy), 0.0).astype(bf16)
        dk = dk + nn(pairs_t, q_h)
        scores_t = jnp.where(rows < cols, nt(k_h, qt), 0.0).astype(bf16)
        dv = dv + nn(scores_t, gy_h)
    vf = v.astype(f32)
    gyf = gy.astype(f32)
    inner = head_sum(gyf * vf, ones)
    dv = dv + head_sum(r * boost * k, ones) * gyf
    dr_ref[0] = (dq * toward + inner * boost * k).astype(bf16)
    dk_ref[0] = (dk * away + inner * boost * r).astype(bf16)
    dv_ref[0] = dv.astype(bf16)
    held = begin.astype(bf16).astype(f32) + jnp.where(blocks, tn(v, kt), 0.0)
    decay = (
        jnp.sum(pos * dq * qt.astype(f32), 0, keepdims=True)
        - jnp.sum((pos + 1.0) * dk * kt.astype(f32), 0, keepdims=True)
        + span * jnp.sum(passed_low.astype(f32) * held, 0, keepdims=True)
    )
    sums_ref[0, 0, 0:1, :] += decay * (-rate)
    sums_ref[0, 0, 1:2, :] += jnp.sum(inner * r * k, 0, keepdims=True)
    carry[...] = passed + jnp.where(blocks, tn(gy, qt), 0.0)


VMEM_LIMIT = 48 * 1024 * 1024


def vec_spec():
    return pl.BlockSpec((1, QUAD), lambda s, q, c: (0, q))


def state_spec():
    return pl.BlockSpec((1, ATTN_WIDTH, QUAD), lambda s, q, c: (s, 0, q))


def sums_spec():
    return pl.BlockSpec((1, 1, 2, QUAD), lambda s, q, c: (s, q, 0, 0))


def sds(shape, dtype):
    return jax.ShapeDtypeStruct(shape, dtype)


def local_state(rate, k, v):
    segs, length, width = k.shape
    block = pl.BlockSpec((1, length, QUAD), lambda s, q: (s, 0, q))
    return pl.pallas_call(
        local_state_kernel,
        grid=(segs, width // QUAD),
        in_specs=[pl.BlockSpec((1, QUAD), lambda s, q: (0, q)), block, block],
        out_specs=pl.BlockSpec((1, ATTN_WIDTH, QUAD), lambda s, q: (s, 0, q)),
        out_shape=sds((segs, ATTN_WIDTH, width), f32),
        compiler_params=pltpu.CompilerParams(vmem_limit_bytes=VMEM_LIMIT),
        name="local_state",
    )(rate, k, v)


def mix_forward(rate, boost, gain, bias, s0, r, k, v, g):
    segs, length, width = r.shape
    span = min(QUAD, length)
    count = length // span
    quads = width // QUAD
    block = pl.BlockSpec((1, span, QUAD), lambda s, q, c: (s, c, q))
    return pl.pallas_call(
        forward_kernel,
        grid=(segs, quads, count),
        in_specs=[vec_spec()] * 4 + [state_spec()] + [block] * 4,
        out_specs=[
            block,
            block,
            pl.BlockSpec((1, 1, ATTN_WIDTH, QUAD), lambda s, q, c: (s, c, 0, q)),
        ],
        out_shape=[
            sds((segs, length, width), bf16),
            sds((segs, length, width), f32),
            sds((segs, count, ATTN_WIDTH, width), f32),
        ],
        scratch_shapes=[pltpu.VMEM((QUAD, QUAD), f32)],
        compiler_params=pltpu.CompilerParams(vmem_limit_bytes=VMEM_LIMIT),
        name="mix_forward",
    )(rate, boost, gain, bias, s0, r, k, v, g)


def gate_back(rate, gain, bias, gz, y, g, r):
    segs, length, width = r.shape
    span = min(QUAD, length)
    quads = width // QUAD
    block = pl.BlockSpec((1, span, QUAD), lambda s, q, c: (s, c, q))
    return pl.pallas_call(
        gate_back_kernel,
        grid=(segs, quads, length // span),
        in_specs=[vec_spec()] * 3 + [block] * 4,
        out_specs=[block, block, state_spec(), sums_spec()],
        out_shape=[
            sds((segs, length, width), bf16),
            sds((segs, length, width), bf16),
            sds((segs, ATTN_WIDTH, width), f32),
            sds((segs, quads, 2, QUAD), f32),
        ],
        scratch_shapes=[pltpu.VMEM((QUAD, QUAD), f32)],
        compiler_params=pltpu.CompilerParams(vmem_limit_bytes=VMEM_LIMIT),
        name="gate_back",
    )(rate, gain, bias, gz, y, g, r)


def mix_backward(rate, boost, end, begin, r, k, v, gy):
    segs, length, width = r.shape
    span = min(QUAD, length)
    count = length // span
    quads = width // QUAD
    block = pl.BlockSpec((1, span, QUAD), lambda s, q, c: (s, count - 1 - c, q))
    return pl.pallas_call(
        backward_kernel,
        grid=(segs, quads, count),
        in_specs=[vec_spec()] * 2
        + [
            state_spec(),
            pl.BlockSpec((1, 1, ATTN_WIDTH, QUAD), lambda s, q, c: (s, count - 1 - c, 0, q)),
        ]
        + [block] * 4,
        out_specs=[block, block, block, sums_spec()],
        out_shape=[sds((segs, length, width), bf16)] * 3 + [sds((segs, quads, 2, QUAD), f32)],
        scratch_shapes=[pltpu.VMEM((QUAD, QUAD), f32)],
        compiler_params=pltpu.CompilerParams(vmem_limit_bytes=VMEM_LIMIT),
        name="mix_backward",
    )(rate, boost, end, begin, r, k, v, gy)


def swap(value, axis):
    return lax.ppermute(value, axis, [(0, 1), (1, 0)])


def send_far(value, team, distance):
    if distance == 1:
        return swap(value, team[-1])
    if distance == 2:
        return swap(value, team[0])
    return lax.ppermute(value, team, [(i, 3 - i) for i in range(4)])


def team_size(team):
    return 2 ** len(team)


def reorder(values, team):
    far = lax.axis_index(team[-1]) == 1
    if len(team) == 1:
        return jnp.where(far, jnp.stack([values[1], values[0]]), values)
    flipped = jnp.stack([values[1], values[0], values[3], values[2]])
    values = jnp.where(far, flipped, values)
    far = lax.axis_index(team[0]) == 1
    flipped = jnp.stack([values[2], values[3], values[0], values[1]])
    return jnp.where(far, flipped, values)


def team_exchange(values, team):
    return [values[0]] + [send_far(values[i], team, i) for i in range(1, team_size(team))]


def abs_exchange(values, team):
    by_distance = reorder(values, team)
    return reorder(jnp.stack(team_exchange(by_distance, team)), team)


def team_copies(value, team):
    if len(team) == 1:
        return [value, swap(value, team[0])]
    near = swap(value, team[1])
    side = swap(value, team[0])
    half = value.shape[0] // 2
    if half == 0:
        return [value, near, side, swap(near, team[0])]
    corner = jnp.concatenate([swap(near[:half], team[0]), swap(side[half:], team[1])], 0)
    return [value, near, side, corner]


def core_pair(value):
    other = swap(value, "c")
    first = lax.axis_index("c") == 0
    return jnp.where(
        first, jnp.concatenate([value, other], 0), jnp.concatenate([other, value], 0)
    )


def gather_tokens(value, team):
    return [core_pair(piece) for piece in team_copies(value, team)]


def core_reduce(part):
    tokens = part.shape[0] // 2
    core = lax.axis_index("c")
    mine = lax.dynamic_slice_in_dim(part, core * tokens, tokens, 0)
    other = lax.dynamic_slice_in_dim(part, (1 - core) * tokens, tokens, 0)
    return mine.astype(f32) + swap(other, "c").astype(f32)


def reduce_tokens(make_part, team):
    if len(team) == 1:
        away = core_reduce(make_part(1)).astype(bf16)
        got = swap(away, team[0])
        return core_reduce(make_part(0)) + got.astype(f32)
    corner = core_reduce(make_part(3)).astype(bf16)
    half = corner.shape[0] // 2
    to_near = swap(corner[:half], team[0])
    to_side = swap(corner[half:], team[1])
    near = core_reduce(make_part(1))
    near = jnp.concatenate([near[:half] + to_near.astype(f32), near[half:]], 0).astype(bf16)
    from_near = swap(near, team[1])
    side = core_reduce(make_part(2))
    side = jnp.concatenate([side[:half], side[half:] + to_side.astype(f32)], 0).astype(bf16)
    from_side = swap(side, team[0])
    return core_reduce(make_part(0)) + from_near.astype(f32) + from_side.astype(f32)


def gather_weights(shards, team, spread):
    n, rows, cols = shards.shape
    members = team_size(team)
    fine = rows // members
    blocks = shards.reshape(n, members, fine, cols).transpose(1, 0, 2, 3)
    mine = abs_exchange(blocks, team)
    whole = lax.all_gather(mine, spread, axis=0, tiled=False)
    nz = lax.axis_size("z")
    nd = whole.shape[0] // nz
    whole = whole.reshape(nd, nz, members, n, fine, cols)
    return whole.transpose(3, 1, 4, 0, 2, 5).reshape(n, nz * fine, nd * members * cols)


def scatter_weights(grads, team, spread):
    n, rows, width = grads.shape
    members = team_size(team)
    nz = lax.axis_size("z")
    nd = lax.axis_size("d")
    fine = rows // nz
    cols = width // (nd * members)
    blocks = grads.reshape(n, nz, fine, nd, members, cols).transpose(3, 1, 4, 0, 2, 5)
    blocks = blocks.reshape(nd * nz, members, n, fine, cols)
    mine = lax.psum_scatter(blocks, spread, scatter_dimension=0, tiled=False)
    mine = abs_exchange(mine, team)
    return mine.transpose(1, 0, 2, 3).reshape(n, members * fine, cols)


def layer_norm(payload_lines, gain, bias):
    center = payload_lines - jnp.mean(payload_lines, -1, keepdims=True)
    inv_scale = lax.rsqrt(jnp.mean(center * center, -1, keepdims=True) + ln_eps)
    normed = center * inv_scale
    return (normed * gain + bias, normed, inv_scale)


def norm_back(upstream_deriv, normed, inv_scale, gain):
    scaled = upstream_deriv * gain
    return inv_scale * (
        scaled
        - jnp.mean(scaled, -1, keepdims=True)
        - normed * jnp.mean(scaled * normed, -1, keepdims=True)
    )


def token_mix(current, earlier, weight):
    return (
        current.astype(f32) * weight + earlier.astype(f32) * (1.0 - weight)
    ).astype(bf16)


def on_device(
    team,
    layer_source,
    piecewise_opening_memory,
    upstream_adjoint,
    earlier_layernorm_scale,
    earlier_layernorm_shift,
    accept_blend,
    lookup_blend,
    payload_blend,
    valve_blend,
    accept_weights,
    lookup_weights,
    payload_weights,
    valve_weights,
    forgetting_loglog,
    diagonal_boost,
    groupwise_scale,
    groupwise_shift,
    emission_weights,
    later_layernorm_scale,
    later_layernorm_shift,
    feedforward_lookup_blend,
    feedforward_accept_blend,
    feedforward_lookup_weights,
    feedforward_payload_weights,
    feedforward_accept_weights,
):
    members = team_size(team)
    every = ("d",) + team + ("z", "c")
    spread = ("d", "z") if lax.axis_size("d") > 1 else "z"
    nz = lax.axis_size("z")
    nd = lax.axis_size("d")
    zi = lax.axis_index("z")
    ci = lax.axis_index("c")
    member = lax.axis_index(team)
    tokens, width = layer_source.shape
    heads_here = nz
    length = 2 * tokens
    line = [(i * 2 + j) for i in range(nz) for j in range(2)]
    down = [(i, i + 1) for i in line[:-1]]
    up = [(i + 1, i) for i in line[:-1]]

    mix_shards = jnp.stack(
        [w.T for w in (accept_weights, lookup_weights, payload_weights, valve_weights)]
    )
    mix_w = gather_weights(mix_shards, team, spread)
    vectors = jnp.stack(
        [
            forgetting_loglog,
            diagonal_boost,
            groupwise_scale.reshape(members, ATTN_WIDTH),
            groupwise_shift.reshape(members, ATTN_WIDTH),
        ]
    )
    vectors = lax.all_gather(vectors, "z", axis=0, tiled=False)
    vectors = lax.dynamic_index_in_dim(vectors, member, 2, keepdims=False)
    vectors = vectors.transpose(1, 0, 2).reshape(4, 1, heads_here * ATTN_WIDTH)
    rate, boost, gn_gain, gn_bias = jnp.exp(vectors[0]), vectors[1], vectors[2], vectors[3]

    residual = layer_source.astype(f32)
    normed1, hat1, inv1 = layer_norm(residual, earlier_layernorm_scale, earlier_layernorm_shift)
    local_x1 = normed1.astype(bf16)
    tail = lax.ppermute(layer_source[-1:], "z", [(i, i + 1) for i in range(nz - 1)])
    tail = jnp.where(ci == 1, tail, swap(tail, "c"))
    halo = layer_norm(tail.astype(f32), earlier_layernorm_scale, earlier_layernorm_shift)[0]
    halo = jnp.where(zi > 0, halo, 0.0).astype(bf16)
    halos = team_copies(halo, team)
    x1 = gather_tokens(local_x1, team)
    whole_x1 = jnp.stack(
        [
            jnp.concatenate([now, jnp.concatenate([edge, now[:-1]], 0)], 1)
            for now, edge in zip(x1, halos)
        ]
    )
    whole_x1 = whole_x1.reshape(members * length, 2 * width)

    nb_cols = emission_weights.shape[1]
    whole_o = lax.all_gather(emission_weights, every, axis=0, tiled=False)
    whole_o = whole_o.reshape(nd * members, nz, 2, members, ATTN_WIDTH, nb_cols)
    whole_o = whole_o.transpose(2, 3, 1, 4, 0, 5).reshape(width, width)
    lookup_t = gather_weights(feedforward_lookup_weights.T[None], team, spread)[0]
    payload_w = gather_weights(feedforward_payload_weights[None], team, spread)[0]
    cr_rows, cr_cols = feedforward_accept_weights.shape
    whole_cr = lax.all_gather(feedforward_accept_weights, every, axis=0, tiled=False)
    whole_cr = whole_cr.reshape(nd * members, nz * 2, cr_rows, cr_cols)
    whole_cr = whole_cr.transpose(0, 2, 1, 3).reshape(width, width)

    blends = jnp.stack([accept_blend, lookup_blend, payload_blend, valve_blend])[:, None, :]
    mix_f = mix_w.astype(f32)
    now_w = (mix_f * blends).astype(bf16)
    past_w = (mix_f * (1.0 - blends)).astype(bf16)
    cols = heads_here * ATTN_WIDTH
    wide_w = jnp.concatenate([now_w, past_w], 2).reshape(4 * cols, 2 * width)
    wide_w, whole_x1 = lax.optimization_barrier((wide_w, whole_x1))
    rkv = nt(whole_x1, wide_w[: 3 * cols]).astype(bf16)
    gate_pre = nt(whole_x1, wide_w[3 * cols :])
    r, k, v = (
        rkv[:, i * cols : (i + 1) * cols].reshape(members, length, cols) for i in range(3)
    )
    gate_pre = gate_pre.reshape(members, length, cols)

    opening = reorder(piecewise_opening_memory[0], team)
    opening = jnp.stack(team_exchange(opening, team))
    opening = lax.all_gather(opening, "z", axis=0, tiled=False)
    opening = opening.transpose(1, 3, 0, 2).reshape(members, ATTN_WIDTH, cols)
    run_ids = jnp.arange(nz)

    def fade(steps):
        return jnp.where(
            steps >= 0, jnp.exp(-rate * (length * jnp.maximum(steps, 0)).astype(f32)), 0.0
        )

    added = local_state(rate, k, v)
    added = lax.all_gather(added, "z", axis=0, tiled=False)
    weight = fade((zi - 1 - run_ids)[:, None])[:, None, None, :]
    s0 = fade(zi[None, None]) * opening + jnp.sum(weight * added, 0)
    z, y, begin = mix_forward(rate, boost, gn_gain, gn_bias, s0, r, k, v, gate_pre)

    got = jnp.stack(team_exchange([z[i] for i in range(members)], team))
    got = reorder(got, team).reshape(members, 2, tokens, cols)
    mine = lax.dynamic_index_in_dim(got, ci, 1, keepdims=False)
    other = swap(lax.dynamic_index_in_dim(got, 1 - ci, 1, keepdims=False), "c")
    pair = jnp.where(ci == 0, jnp.stack([mine, other]), jnp.stack([other, mine]))
    z_rows = pair.transpose(2, 0, 1, 3).reshape(tokens, width)
    middle = residual + nn(z_rows, whole_o)

    normed2, hat2, inv2 = layer_norm(middle, later_layernorm_scale, later_layernorm_shift)
    local_x2 = normed2.astype(bf16)
    edge2 = lax.ppermute(local_x2[-1:], ("z", "c"), down)
    prev2 = jnp.concatenate([edge2, local_x2[:-1]], 0)
    mixed_ck = token_mix(local_x2, prev2, feedforward_lookup_blend)
    mixed_cr = token_mix(local_x2, prev2, feedforward_accept_blend)
    seq_ck = gather_tokens(mixed_ck, team)
    key_pre = [nt(piece, lookup_t) for piece in seq_ck]
    key_relu = [jax.nn.relu(piece) for piece in key_pre]
    key_sq = [jnp.square(piece).astype(bf16) for piece in key_relu]
    key_relu = [piece.astype(bf16) for piece in key_relu]
    value_sum = reduce_tokens(lambda i: nn(key_sq[i], payload_w).astype(bf16), team)
    sig_two = jax.nn.sigmoid(nn(mixed_cr, whole_cr))
    block_out = (middle + sig_two * value_sum).astype(bf16)

    cot = upstream_adjoint.astype(f32)
    grad_value = (cot * sig_two).astype(bf16)
    grad_r2 = (cot * value_sum * sig_two * (1.0 - sig_two)).astype(bf16)
    seq_gv = gather_tokens(grad_value, team)
    grad_key = [
        (nt(piece, payload_w) * (2.0 * held.astype(f32))).astype(bf16)
        for piece, held in zip(seq_gv, key_relu)
    ]
    grad_ck = reduce_tokens(lambda i: nn(grad_key[i], lookup_t).astype(bf16), team)
    grad_cr = nt(grad_r2, whole_cr)
    cv_part = tn(jnp.concatenate(key_sq, 0), jnp.concatenate(seq_gv, 0)).astype(bf16)
    chan_value_grad = scatter_weights(cv_part[None], team, spread)[0].astype(f32)
    ck_part = tn(jnp.concatenate(grad_key, 0), jnp.concatenate(seq_ck, 0)).astype(bf16)
    chan_key_grad = scatter_weights(ck_part[None], team, spread)[0].T.astype(f32)
    cr_part = tn(mixed_cr, grad_r2).astype(bf16)
    cr_part = cr_part.reshape(nd * members, cr_rows, nz * 2, cr_cols).transpose(0, 2, 1, 3)
    cr_part = cr_part.reshape(nd * members * nz * 2, cr_rows, cr_cols)
    chan_recept_grad = lax.psum_scatter(cr_part, every, scatter_dimension=0, tiled=False).astype(
        f32
    )
    spread_two = local_x2.astype(f32) - prev2.astype(f32)
    chan_mix_k_part = jnp.sum(grad_ck * spread_two, 0)
    chan_mix_r_part = jnp.sum(grad_cr * spread_two, 0)
    delayed_two = grad_ck * (1.0 - feedforward_lookup_blend) + grad_cr * (
        1.0 - feedforward_accept_blend
    )
    edge_up = lax.ppermute(delayed_two[:1], ("z", "c"), up)
    grad_x2 = (
        grad_ck * feedforward_lookup_blend
        + grad_cr * feedforward_accept_blend
        + jnp.concatenate([delayed_two[1:], edge_up], 0)
    )
    ln2_gain_part = jnp.sum(grad_x2 * hat2, 0)
    ln2_bias_part = jnp.sum(grad_x2, 0)
    grad_middle = cot + norm_back(grad_x2, hat2, inv2, later_layernorm_scale)
    grad_mix = grad_middle.astype(bf16)

    grad_z = nt(grad_mix, whole_o).astype(bf16)
    o_part = tn(z_rows, grad_mix).astype(bf16)
    o_part = o_part.reshape(2, members, nz, ATTN_WIDTH, nd * members, nb_cols)
    o_part = o_part.transpose(4, 2, 0, 1, 3, 5).reshape(
        nd * members * nz * 2, members * ATTN_WIDTH, nb_cols
    )
    weight_o_grad = lax.psum_scatter(o_part, every, scatter_dimension=0, tiled=False).astype(f32)
    grad_z = grad_z.reshape(tokens, 2, members, cols).transpose(1, 2, 0, 3)
    mine = lax.dynamic_index_in_dim(grad_z, ci, 0, keepdims=False)
    other = swap(lax.dynamic_index_in_dim(grad_z, 1 - ci, 0, keepdims=False), "c")
    pair = jnp.where(ci == 0, jnp.stack([mine, other], 1), jnp.stack([other, mine], 1))
    pair = reorder(pair.reshape(members, length, cols), team)
    grad_z = jnp.stack(team_exchange(pair, team))

    grad_gate, grad_y, added, gn_sums = gate_back(
        rate, gn_gain, gn_bias, grad_z, y, gate_pre, r
    )
    added = lax.all_gather(added, "z", axis=0, tiled=False)
    weight = fade((run_ids - zi - 1)[:, None])[:, None, None, :]
    end = jnp.sum(weight * added, 0)
    dr, dk, dv, mix_sums = mix_backward(rate, boost, end, begin, r, k, v, grad_y)
    first = jnp.sum(fade(run_ids[:, None])[:, None, None, :] * added, 0)
    first = lax.dynamic_slice_in_dim(first, zi * ATTN_WIDTH, ATTN_WIDTH, 2)
    first = reorder(jnp.stack(team_exchange(first, team)), team)
    initial_state_gradient = first.transpose(0, 2, 1)[None]

    grads = jnp.concatenate([dr, dk, dv, grad_gate], 2)
    edge = lax.ppermute(grads[:, :1], "z", [(i + 1, i) for i in range(nz - 1)])
    both = jnp.concatenate([grads, jnp.concatenate([grads[:, 1:], edge], 1)], 2)
    tall_w = jnp.concatenate([now_w, past_w], 0).reshape(8 * cols, width)
    tall_w, both = lax.optimization_barrier((tall_w, both))
    grad_x1 = reduce_tokens(lambda i: nn(both[i], tall_w).astype(bf16), team)
    wide_part = tn(grads.reshape(members * length, 4 * cols), whole_x1)
    wide_part = wide_part.reshape(4, cols, 2, width)
    now_part, past_part = wide_part[:, :, 0], wide_part[:, :, 1]
    mix_parts = jnp.sum(mix_f * (now_part - past_part), 1)
    weight_parts = (now_part * blends + past_part * (1.0 - blends)).astype(bf16)
    weight_grads = scatter_weights(weight_parts, team, spread)
    weight_r_grad, weight_k_grad, weight_v_grad, weight_g_grad = (
        weight_grads[i].T.astype(f32) for i in range(4)
    )
    ln1_gain_part = jnp.sum(grad_x1 * hat1, 0)
    ln1_bias_part = jnp.sum(grad_x1, 0)
    in_grad = grad_middle + norm_back(grad_x1, hat1, inv1, earlier_layernorm_scale)

    by_head = jnp.stack(
        [
            jnp.sum(gn_sums[:, :, 0], 0),
            jnp.sum(gn_sums[:, :, 1], 0),
            jnp.sum(mix_sums[:, :, 0], 0),
            jnp.sum(mix_sums[:, :, 1], 0),
        ]
    ).reshape(4, nz, 1, 1, ATTN_WIDTH)
    placed = lax.dynamic_update_slice(
        jnp.zeros((4, nz, 2, members, ATTN_WIDTH), f32), by_head, (0, 0, ci, member, 0)
    ).reshape(4, width)
    small = jnp.concatenate(
        [
            mix_parts,
            placed,
            jnp.stack(
                [
                    ln1_gain_part,
                    ln1_bias_part,
                    ln2_gain_part,
                    ln2_bias_part,
                    chan_mix_k_part,
                    chan_mix_r_part,
                ]
            ),
        ],
        0,
    )
    small = lax.psum(small, every)
    here = lax.dynamic_slice_in_dim(
        small[4:8].reshape(4, nz * 2, members * ATTN_WIDTH), zi * 2 + ci, 1, 1
    )[:, 0]
    per_head = here.reshape(4, members, ATTN_WIDTH)
    return (
        block_out,
        in_grad,
        initial_state_gradient,
        small[8],
        small[9],
        small[0],
        small[1],
        small[2],
        small[3],
        weight_r_grad,
        weight_k_grad,
        weight_v_grad,
        weight_g_grad,
        per_head[2],
        per_head[3],
        here[0],
        here[1],
        weight_o_grad,
        small[10],
        small[11],
        small[12],
        small[13],
        chan_key_grad,
        chan_value_grad,
        chan_recept_grad,
    )


def solution(mesh):
    nb, nh = mesh.shape["batch"], mesh.shape["head"]

    def whole(*args):
        attn_count = args[13].shape[0]
        members = attn_count // nh
        team = ("t1", "t0") if members == 4 else ("t0",)
        fine = Mesh(
            mesh.devices.reshape((nb // members,) + (2,) * len(team) + (nh // 2, 2)),
            ("d",) + team + ("z", "c"),
        )
        batch = ("d",) + team
        head = ("z", "c")
        tok = P(batch + head, None)
        state = P(batch, head, None, None)
        cols = P(batch, head)
        rows = P(head, batch)
        per_head = P(head, None)
        channel = P(head)
        same = P()
        in_specs = (
            (tok, state, tok)
            + (same,) * 6
            + (cols,) * 4
            + (per_head,) * 2
            + (channel,) * 2
            + (rows,)
            + (same,) * 4
            + (cols, rows, cols)
        )
        out_specs = (
            (tok, tok, state)
            + (same,) * 6
            + (cols,) * 4
            + (per_head,) * 2
            + (channel,) * 2
            + (rows,)
            + (same,) * 4
            + (cols, rows, cols)
        )
        return jax.shard_map(
            functools.partial(on_device, team),
            mesh=fine,
            in_specs=in_specs,
            out_specs=out_specs,
            check_vma=False,
        )(*args)

    return whole
```

```python
import functools

import jax
import jax.numpy as jnp
from jax import lax
from jax.experimental import pallas as pl
from jax.experimental.pallas import tpu as pltpu
from jax.sharding import Mesh
from jax.sharding import PartitionSpec as P

ATTN_WIDTH = 64
QUAD = 256

ln_eps = 1e-05
gn_eps = 0.00064
f32 = jnp.float32
bf16 = jnp.bfloat16


def nn(left, right):
    return jnp.dot(left, right, preferred_element_type=f32)


def nt(left, right):
    return lax.dot_general(left, right, (((1,), (1,)), ((), ())), preferred_element_type=f32)


def tn(left, right):
    return lax.dot_general(left, right, (((0,), (0,)), ((), ())), preferred_element_type=f32)


def head_masks():
    lane_head = lax.broadcasted_iota(jnp.int32, (1, QUAD), 1) // ATTN_WIDTH
    return [lane_head == h for h in range(QUAD // ATTN_WIDTH)]


def block_mask():
    row_head = lax.broadcasted_iota(jnp.int32, (QUAD, QUAD), 0) // ATTN_WIDTH
    col_head = lax.broadcasted_iota(jnp.int32, (QUAD, QUAD), 1) // ATTN_WIDTH
    return row_head == col_head


def only(mask, lines):
    return jnp.where(mask, lines, jnp.zeros_like(lines))


def compress(square, masks):
    return sum(
        jnp.where(m, square[h * ATTN_WIDTH : (h + 1) * ATTN_WIDTH, :], 0.0)
        for h, m in enumerate(masks)
    )


def expand(packed, blocks):
    return jnp.where(blocks, jnp.concatenate([packed] * (QUAD // ATTN_WIDTH), 0), 0.0)


def head_sum(lines, ones):
    return nn(lines.astype(bf16), ones)


def head_sum_fine(lines, ones):
    coarse = lines.astype(bf16)
    return nn(coarse, ones) + nn((lines - coarse.astype(f32)).astype(bf16), ones)


def local_state_kernel(rate_ref, k_ref, v_ref, out_ref):
    length = k_ref.shape[1]
    rate = rate_ref[...]
    remaining = (length - 1) - lax.broadcasted_iota(jnp.int32, (length, 1), 0)
    faded = (k_ref[0].astype(f32) * jnp.exp(-rate * remaining.astype(f32))).astype(bf16)
    out_ref[0] = compress(tn(v_ref[0], faded), head_masks())


def group_norm_parts(y, ones):
    center = y - head_sum_fine(y, ones) * (1.0 / ATTN_WIDTH)
    inv = lax.rsqrt(head_sum(center * center, ones) * (1.0 / ATTN_WIDTH) + gn_eps)
    return center * inv, inv


def forward_kernel(
    rate_ref, boost_ref, gain_ref, bias_ref, s0_ref, r_ref, k_ref, v_ref, g_ref,
    z_ref, y_ref, begin_ref, state,
):
    span = r_ref.shape[1]
    masks = head_masks()
    blocks = block_mask()
    ones = jnp.where(blocks, 1.0, 0.0).astype(bf16)

    @pl.when(pl.program_id(2) == 0)
    def _():
        state[...] = expand(s0_ref[0], blocks)

    rate = rate_ref[...]
    pos = lax.broadcasted_iota(jnp.int32, (span, 1), 0).astype(f32)
    r = r_ref[0].astype(f32)
    k = k_ref[0].astype(f32)
    v = v_ref[0]
    qt = (r * jnp.exp(-rate * pos)).astype(bf16)
    kt = (k * jnp.exp(rate * (pos + 1.0))).astype(bf16)
    begin = state[...]
    begin_ref[0, 0] = compress(begin, masks)
    y = nt(qt, begin.astype(bf16))
    causal = lax.broadcasted_iota(jnp.int32, (span, span), 0) > lax.broadcasted_iota(
        jnp.int32, (span, span), 1
    )
    for m in masks:
        scores = jnp.where(causal, nt(only(m, qt), kt), 0.0).astype(bf16)
        y = y + nn(scores, only(m, v))
    y = y + head_sum(r * boost_ref[...] * k, ones) * v.astype(f32)
    state[...] = jnp.exp(-rate * span) * (begin + jnp.where(blocks, tn(v, kt), 0.0))
    y_ref[0] = y
    normed, _ = group_norm_parts(y, ones)
    g = g_ref[0]
    z_ref[0] = ((normed * gain_ref[...] + bias_ref[...]) * (g * jax.nn.sigmoid(g))).astype(bf16)


def gate_back_kernel(
    rate_ref, gain_ref, bias_ref, gz_ref, y_ref, g_ref, r_ref,
    gg_ref, gy_ref, end_ref, sums_ref, total,
):
    span = r_ref.shape[1]
    step = pl.program_id(2)
    blocks = block_mask()
    ones = jnp.where(blocks, 1.0, 0.0).astype(bf16)

    @pl.when(step == 0)
    def _():
        total[...] = jnp.zeros_like(total)
        sums_ref[...] = jnp.zeros_like(sums_ref)

    normed, inv = group_norm_parts(y_ref[0], ones)
    gain = gain_ref[...]
    g = g_ref[0]
    gz = gz_ref[0].astype(f32)
    sig = jax.nn.sigmoid(g)
    grad_grouped = gz * (g * sig)
    grouped = normed * gain + bias_ref[...]
    gg_ref[0] = (gz * grouped * sig * (1.0 + g * (1.0 - sig))).astype(bf16)
    sums_ref[0, 0, 0:1, :] += jnp.sum(grad_grouped * normed, 0, keepdims=True)
    sums_ref[0, 0, 1:2, :] += jnp.sum(grad_grouped, 0, keepdims=True)
    e = grad_grouped * gain
    gy = inv * (
        e
        - head_sum_fine(e, ones) * (1.0 / ATTN_WIDTH)
        - normed * (head_sum(e * normed, ones) * (1.0 / ATTN_WIDTH))
    )
    gy = gy.astype(bf16)
    gy_ref[0] = gy
    pos = (lax.broadcasted_iota(jnp.int32, (span, 1), 0) + step * span).astype(f32)
    faded = (r_ref[0].astype(f32) * jnp.exp(-rate_ref[...] * pos)).astype(bf16)
    total[...] += tn(gy, faded)
    end_ref[0] = compress(total[...], head_masks())


def backward_kernel(
    rate_ref, boost_ref, end_ref, begin_ref, r_ref, k_ref, v_ref, gy_ref,
    dr_ref, dk_ref, dv_ref, sums_ref, carry,
):
    span = r_ref.shape[1]
    masks = head_masks()
    blocks = block_mask()
    ones = jnp.where(blocks, 1.0, 0.0).astype(bf16)

    @pl.when(pl.program_id(2) == 0)
    def _():
        carry[...] = expand(end_ref[0], blocks)
        sums_ref[...] = jnp.zeros_like(sums_ref)

    rate = rate_ref[...]
    boost = boost_ref[...]
    pos = lax.broadcasted_iota(jnp.int32, (span, 1), 0).astype(f32)
    toward = jnp.exp(-rate * pos)
    away = jnp.exp(rate * (pos + 1.0))
    r = r_ref[0].astype(f32)
    k = k_ref[0].astype(f32)
    v = v_ref[0]
    gy = gy_ref[0]
    qt = (r * toward).astype(bf16)
    kt = (k * away).astype(bf16)
    passed = jnp.exp(-rate * span) * carry[...]
    passed_low = passed.astype(bf16)
    begin = expand(begin_ref[0, 0], blocks)
    rows = lax.broadcasted_iota(jnp.int32, (span, span), 0)
    cols = lax.broadcasted_iota(jnp.int32, (span, span), 1)
    dq = nn(gy, begin.astype(bf16))
    dk = nn(v, passed_low)
    dv = nt(kt, passed_low)
    for m in masks:
        v_h, gy_h, k_h, q_h = only(m, v), only(m, gy), only(m, kt), only(m, qt)
        pairs = jnp.where(rows > cols, nt(gy_h, v), 0.0).astype(bf16)
        dq = dq + nn(pairs, k_h)
        pairs_t = jnp.where(rows < cols, nt(v_h, gy), 0.0).astype(bf16)
        dk = dk + nn(pairs_t, q_h)
        scores_t = jnp.where(rows < cols, nt(k_h, qt), 0.0).astype(bf16)
        dv = dv + nn(scores_t, gy_h)
    vf = v.astype(f32)
    gyf = gy.astype(f32)
    inner = head_sum(gyf * vf, ones)
    dv = dv + head_sum(r * boost * k, ones) * gyf
    dr_ref[0] = (dq * toward + inner * boost * k).astype(bf16)
    dk_ref[0] = (dk * away + inner * boost * r).astype(bf16)
    dv_ref[0] = dv.astype(bf16)
    held = begin.astype(bf16).astype(f32) + jnp.where(blocks, tn(v, kt), 0.0)
    decay = (
        jnp.sum(pos * dq * qt.astype(f32), 0, keepdims=True)
        - jnp.sum((pos + 1.0) * dk * kt.astype(f32), 0, keepdims=True)
        + span * jnp.sum(passed_low.astype(f32) * held, 0, keepdims=True)
    )
    sums_ref[0, 0, 0:1, :] += decay * (-rate)
    sums_ref[0, 0, 1:2, :] += jnp.sum(inner * r * k, 0, keepdims=True)
    carry[...] = passed + jnp.where(blocks, tn(gy, qt), 0.0)


VMEM_LIMIT = 56 * 1024 * 1024
params = pltpu.CompilerParams(vmem_limit_bytes=VMEM_LIMIT)


def lasts(microseconds):
    return pl.CostEstimate(
        flops=int(FLOPS_PER_US * microseconds), bytes_accessed=0, transcendentals=0
    )


FLOPS_PER_US = 3e9


def vec_spec():
    return pl.BlockSpec((1, QUAD), lambda s, q, c: (0, q))


def state_spec():
    return pl.BlockSpec((1, ATTN_WIDTH, QUAD), lambda s, q, c: (s, 0, q))


def sums_spec():
    return pl.BlockSpec((1, 1, 2, QUAD), lambda s, q, c: (s, q, 0, 0))


def sds(shape, dtype):
    return jax.ShapeDtypeStruct(shape, dtype)


def local_state(rate, rkv):
    _, segs, length, width = rkv.shape

    def block(i):
        return pl.BlockSpec((None, 1, length, QUAD), lambda s, q: (i, s, 0, q))

    return pl.pallas_call(
        local_state_kernel,
        grid=(segs, width // QUAD),
        in_specs=[pl.BlockSpec((1, QUAD), lambda s, q: (0, q)), block(1), block(2)],
        out_specs=pl.BlockSpec((1, ATTN_WIDTH, QUAD), lambda s, q: (s, 0, q)),
        out_shape=sds((segs, ATTN_WIDTH, width), f32),
        compiler_params=params,
        cost_estimate=lasts(5),
        name="local_state",
    )(rate, rkv, rkv)


def mix_forward(rate, boost, gain, bias, s0, rkv, g):
    _, segs, length, width = rkv.shape
    span = min(QUAD, length)
    count = length // span
    quads = width // QUAD
    block = pl.BlockSpec((1, span, QUAD), lambda s, q, c: (s, c, q))

    def part(i):
        return pl.BlockSpec((None, 1, span, QUAD), lambda s, q, c: (i, s, c, q))

    return pl.pallas_call(
        forward_kernel,
        grid=(segs, quads, count),
        in_specs=[vec_spec()] * 4
        + [state_spec(), part(0), part(1), part(2), block],
        out_specs=[
            block,
            block,
            pl.BlockSpec((1, 1, ATTN_WIDTH, QUAD), lambda s, q, c: (s, c, 0, q)),
        ],
        out_shape=[
            sds((segs, length, width), bf16),
            sds((segs, length, width), f32),
            sds((segs, count, ATTN_WIDTH, width), f32),
        ],
        scratch_shapes=[pltpu.VMEM((QUAD, QUAD), f32)],
        compiler_params=params,
        cost_estimate=lasts(20),
        name="mix_forward",
    )(rate, boost, gain, bias, s0, rkv, rkv, rkv, g)


def gate_back(rate, gain, bias, gz, y, g, rkv):
    _, segs, length, width = rkv.shape
    span = min(QUAD, length)
    quads = width // QUAD
    block = pl.BlockSpec((1, span, QUAD), lambda s, q, c: (s, c, q))
    lead = pl.BlockSpec((None, 1, span, QUAD), lambda s, q, c: (0, s, c, q))
    return pl.pallas_call(
        gate_back_kernel,
        grid=(segs, quads, length // span),
        in_specs=[vec_spec()] * 3 + [block, block, block, lead],
        out_specs=[block, block, state_spec(), sums_spec()],
        out_shape=[
            sds((segs, length, width), bf16),
            sds((segs, length, width), bf16),
            sds((segs, ATTN_WIDTH, width), f32),
            sds((segs, quads, 2, QUAD), f32),
        ],
        scratch_shapes=[pltpu.VMEM((QUAD, QUAD), f32)],
        compiler_params=params,
        cost_estimate=lasts(18 / 8),
        name="gate_back",
    )(rate, gain, bias, gz, y, g, rkv)


def mix_backward(rate, boost, end, begin, rkv, gy):
    _, segs, length, width = rkv.shape
    span = min(QUAD, length)
    count = length // span
    quads = width // QUAD
    block = pl.BlockSpec((1, span, QUAD), lambda s, q, c: (s, count - 1 - c, q))

    def part(i):
        return pl.BlockSpec((None, 1, span, QUAD), lambda s, q, c: (i, s, count - 1 - c, q))

    return pl.pallas_call(
        backward_kernel,
        grid=(segs, quads, count),
        in_specs=[vec_spec()] * 2
        + [
            state_spec(),
            pl.BlockSpec((1, 1, ATTN_WIDTH, QUAD), lambda s, q, c: (s, count - 1 - c, 0, q)),
        ]
        + [part(0), part(1), part(2), block],
        out_specs=[block, block, block, sums_spec()],
        out_shape=[sds((segs, length, width), bf16)] * 3 + [sds((segs, quads, 2, QUAD), f32)],
        scratch_shapes=[pltpu.VMEM((QUAD, QUAD), f32)],
        compiler_params=params,
        cost_estimate=lasts(29 / 8),
        name="mix_backward",
    )(rate, boost, end, begin, rkv, rkv, rkv, gy)


def project_kernel(core_ref, x_ref, halo_ref, w_ref, rkv_ref, gate_ref, carry):
    x = x_ref[...]
    now_w = w_ref[0].reshape(-1, x.shape[1])
    past_w = w_ref[1].reshape(-1, x.shape[1])
    now = nt(x, now_w)
    past = nt(x, past_w)

    @pl.when(pl.program_id(1) == 0)
    def _():
        carry[...] = nt(halo_ref[...], past_w)

    rows = lax.broadcasted_iota(jnp.int32, past.shape, 0)
    out = now + jnp.where(rows == 0, carry[0:1, :], pltpu.roll(past, 1, 0))
    cols = gate_ref.shape[1]
    for i in range(3):
        rkv_ref[i] = out[:, i * cols : (i + 1) * cols].astype(bf16)
    gate_ref[...] = out[:, 3 * cols :]
    carry[0:1, :] = past[past.shape[0] - 1 :, :]


def project(core, x, halos, weights):
    segs, _, tokens, width = x.shape
    cols = weights.shape[2]
    spec = pltpu.PrefetchScalarGridSpec(
        num_scalar_prefetch=1,
        grid=(segs, 2),
        in_specs=[
            pl.BlockSpec((None, None, tokens, width), lambda s, h, core: (s, h ^ core[0], 0, 0)),
            pl.BlockSpec((None, 8, width), lambda s, h, core: (s, 0, 0)),
            pl.BlockSpec((2, 4, cols, width), lambda s, h, core: (0, 0, 0, 0)),
        ],
        out_specs=[
            pl.BlockSpec((3, None, tokens, cols), lambda s, h, core: (0, s, h, 0)),
            pl.BlockSpec((None, tokens, cols), lambda s, h, core: (s, h, 0)),
        ],
        scratch_shapes=[pltpu.VMEM((8, 4 * cols), f32)],
    )
    return pl.pallas_call(
        project_kernel,
        grid_spec=spec,
        out_shape=[
            sds((3, segs, 2 * tokens, cols), bf16),
            sds((segs, 2 * tokens, cols), f32),
        ],
        compiler_params=params,
        cost_estimate=lasts(50),
        name="project",
    )(core, x, halos, weights)


def project_back_kernel(core_ref, r_ref, k_ref, v_ref, g_ref, edge_ref, w_ref, out_ref, carry):
    refs = (r_ref, k_ref, v_ref, g_ref)
    tokens = r_ref.shape[0]
    now = jnp.concatenate([ref[...] for ref in refs], 1)

    @pl.when(pl.program_id(0) == 0)
    def _():
        carry[...] = jnp.concatenate([edge_ref[i] for i in range(4)], 1).astype(f32)

    wide = now.astype(f32)
    rows = lax.broadcasted_iota(jnp.int32, wide.shape, 0)
    later = jnp.where(rows == tokens - 1, carry[0:1, :], pltpu.roll(wide, tokens - 1, 0))
    carry[0:1, :] = wide[0:1, :]
    both = jnp.concatenate([now, later.astype(bf16)], 1)
    out_ref[...] = nn(both, w_ref[...]).astype(bf16)


def project_back(core, seg, grads, edges, weights):
    segs, length, cols = grads[0].shape
    tokens = length // 2
    width = weights.shape[3]
    block = pl.BlockSpec((None, tokens, cols), lambda h, core: (seg, 1 - h, 0))
    spec = pltpu.PrefetchScalarGridSpec(
        num_scalar_prefetch=1,
        grid=(2,),
        in_specs=[block] * 4
        + [
            pl.BlockSpec((None, 4, 8, cols), lambda h, core: (seg, 0, 0, 0)),
            pl.BlockSpec((8 * cols, width), lambda h, core: (0, 0)),
        ],
        out_specs=pl.BlockSpec((None, tokens, width), lambda h, core: ((1 - h) ^ core[0], 0, 0)),
        scratch_shapes=[pltpu.VMEM((8, 4 * cols), f32)],
    )
    return pl.pallas_call(
        project_back_kernel,
        grid_spec=spec,
        out_shape=sds((2, tokens, width), bf16),
        compiler_params=params,
        cost_estimate=lasts(14 / 8),
        name="project_back",
    )(core, *grads, edges, weights.reshape(8 * cols, width))


def mix_weight_kernel(count, core_ref, *refs):
    grads, (edge_ref, x_ref, w_ref, blend_ref) = refs[:count], refs[count : count + 4]
    out_ref, mix_ref, flat, total = refs[count + 4 :]
    group, tile = pl.program_id(0), pl.program_id(1)
    segs, length, cols = grads[0].shape
    tokens = length // 2

    @pl.when(tile == 0)
    def _():
        for s in range(segs):
            for i, ref in enumerate(grads):
                here = ref[s].astype(f32)
                rows = lax.broadcasted_iota(jnp.int32, here.shape, 0)
                later = jnp.where(
                    rows == length - 1,
                    edge_ref[s, i, 0:1, :].astype(f32),
                    pltpu.roll(here, length - 1, 0),
                )
                for h in range(2):
                    at = pl.multiple_of((2 * s + (h ^ core_ref[0])) * tokens, tokens)
                    part = slice(h * tokens, (h + 1) * tokens)
                    flat[i * cols : (i + 1) * cols, pl.ds(at, tokens)] = here[part].T.astype(bf16)
                    flat[(count + i) * cols : (count + i + 1) * cols, pl.ds(at, tokens)] = (
                        later[part].T.astype(bf16)
                    )

    got = nn(flat[...], x_ref[...].reshape(segs * length, x_ref.shape[3]))
    final = group == pl.num_programs(0) - 1

    @pl.when(jnp.logical_and(group == 0, jnp.logical_not(final)))
    def _():
        total[tile] = got

    @pl.when(jnp.logical_and(group > 0, jnp.logical_not(final)))
    def _():
        total[tile] += got

    @pl.when(final)
    def _():
        whole = jnp.where(group == 0, 0.0, total[tile]) + got
        nz, fine = out_ref.shape[0], out_ref.shape[2]
        for i in range(count):
            a = whole[i * cols : (i + 1) * cols]
            b = whole[(count + i) * cols : (count + i + 1) * cols]
            blend = blend_ref[i]
            grad = (a * blend + b * (1.0 - blend)).astype(bf16)
            mix_ref[i] = jnp.sum(w_ref[i].astype(f32) * (a - b), 0, keepdims=True)
            for z in range(nz):
                out_ref[z, i] = grad[z * fine : (z + 1) * fine]


def mix_weight_grads(core, grads, edges, x, plain, blends, nd, members, nz):
    count = len(grads)
    segs, length, cols = grads[0].shape
    tokens = length // 2
    width = x.shape[3]
    tiles = nd * members
    tile = width // tiles
    fine = cols // nz
    groups = segs // 2
    block = pl.BlockSpec((2, length, cols), lambda t, n, core: (t, 0, 0))

    def last(t, n):
        return jnp.where(t == groups - 1, n, 0)

    spec = pltpu.PrefetchScalarGridSpec(
        num_scalar_prefetch=1,
        grid=(groups, tiles),
        in_specs=[block] * count
        + [
            pl.BlockSpec((2, count, 8, cols), lambda t, n, core: (t, 0, 0, 0)),
            pl.BlockSpec((2, 2, tokens, tile), lambda t, n, core: (t, 0, 0, n)),
            pl.BlockSpec((count, cols, tile), lambda t, n, core: (0, 0, last(t, n))),
            pl.BlockSpec((count, 1, tile), lambda t, n, core: (0, 0, last(t, n))),
        ],
        out_specs=[
            pl.BlockSpec(
                (None, nz, None, count, fine, tile),
                lambda t, n, core: (last(t, n) // members, 0, last(t, n) % members, 0, 0, 0),
            ),
            pl.BlockSpec((count, 1, tile), lambda t, n, core: (0, 0, last(t, n))),
        ],
        scratch_shapes=[
            pltpu.VMEM((2 * count * cols, 2 * length), bf16),
            pltpu.VMEM((tiles, 2 * count * cols, tile), f32),
        ],
    )
    return pl.pallas_call(
        functools.partial(mix_weight_kernel, count),
        grid_spec=spec,
        out_shape=[
            sds((nd, nz, members, count, fine, tile), bf16),
            sds((count, 1, width), f32),
        ],
        compiler_params=params,
        cost_estimate=lasts(13 * count / 8),
        name="mix_weight_grads",
    )(core, *grads, edges, x, plain, blends[:, None, :])


def outer_kernel(count, *refs):
    lefts, rights = refs[:count], refs[count : 2 * count]
    out_ref, flat, total = refs[2 * count :]
    group, tile = pl.program_id(0), pl.program_id(1)
    length = lefts[0].shape[0]
    final = group == count // 2 - 1
    for i in range(count // 2):

        @pl.when(group == i)
        def _(i=i):
            @pl.when(tile == 0)
            def _():
                flat[:, :length] = lefts[2 * i][...].T
                flat[:, length:] = lefts[2 * i + 1][...].T

            got = nn(flat[...], jnp.concatenate([rights[2 * i][...], rights[2 * i + 1][...]], 0))
            if i > 0:
                got = got + total[tile]
            if i < count // 2 - 1:
                total[tile] = got
            else:
                nz, fine = out_ref.shape[0], out_ref.shape[2]
                low = got.astype(bf16)
                for z in range(nz):
                    out_ref[z, 0] = low[z * fine : (z + 1) * fine, :]


def outer_grads(lefts, rights, nd, members, nz):
    length, rows = lefts[0].shape
    width = rights[0].shape[1]
    tiles = nd * members
    tile = width // tiles
    fine = rows // nz
    count = len(lefts)
    groups = count // 2

    def right(i):
        def index(t, n):
            return 0, jnp.where(t < i // 2, 0, jnp.where(t > i // 2, tiles - 1, n))

        return pl.BlockSpec((length, tile), index)

    def last(t, n):
        return jnp.where(t == groups - 1, n, 0)

    return pl.pallas_call(
        functools.partial(outer_kernel, count),
        grid=(groups, tiles),
        in_specs=[pl.BlockSpec((length, rows), lambda t, n: (0, 0))] * count
        + [right(i) for i in range(count)],
        out_specs=pl.BlockSpec(
            (None, nz, None, 1, fine, tile),
            lambda t, n: (last(t, n) // members, 0, last(t, n) % members, 0, 0, 0),
        ),
        out_shape=sds((nd, nz, members, 1, fine, tile), bf16),
        scratch_shapes=[
            pltpu.VMEM((rows, 2 * length), bf16),
            pltpu.VMEM((tiles, rows, tile), f32),
        ],
        compiler_params=params,
        cost_estimate=lasts(25 / 8),
        name="outer_grads",
    )(*lefts, *rights)


def side_kernel(nd, nz, where_ref, z_ref, gm_ref, gr_ref, cr_ref, out_ref, z_flat, gr_flat):
    distance = pl.program_id(0)
    members = pl.num_programs(0)
    core, member = where_ref[0], where_ref[1]
    width = z_ref.shape[1]
    cols = width // (nd * members)
    half = width // 2
    head = half // nz

    @pl.when(distance == 0)
    def _():
        z_flat[...] = z_ref[...].T
        for c in range(2):
            for z in range(nz):
                at = (2 * z + c) * head
                gr_flat[c * half + z * head : c * half + (z + 1) * head, :] = (
                    gr_ref[:, at : at + head].T
                )

    for d in range(nd):
        at = pl.multiple_of((d * members + (member ^ distance)) * cols, cols)
        for i, (flat, right) in enumerate(((z_flat, gm_ref), (gr_flat, cr_ref))):
            got = nn(flat[...], right[:, pl.ds(at, cols)]).astype(bf16)
            place = slice(i * nd * cols + d * cols, i * nd * cols + (d + 1) * cols)
            for c in range(2):
                out_ref[c ^ core, :, place] = got[c * half : (c + 1) * half]


def side_grads(where, z_rows, grad_mix, grad_r2, mixed_cr, nd, members, nz):
    tokens, width = z_rows.shape
    wide = width // members
    whole = pl.BlockSpec((tokens, width), lambda i, where: (0, 0))
    out = pl.pallas_call(
        functools.partial(side_kernel, nd, nz),
        grid_spec=pltpu.PrefetchScalarGridSpec(
            num_scalar_prefetch=1,
            grid=(members,),
            in_specs=[whole] * 4,
            out_specs=pl.BlockSpec(
                (None, 2, width // 2, 2 * wide), lambda i, where: (i, 0, 0, 0)
            ),
            scratch_shapes=[pltpu.VMEM((width, tokens), bf16)] * 2,
        ),
        out_shape=sds((members, 2, width // 2, 2 * wide), bf16),
        compiler_params=params,
        cost_estimate=lasts(17 / 8),
        name="side_grads",
    )(where, z_rows, grad_mix, grad_r2, mixed_cr)
    return out.reshape(members, width, 2 * wide)


def place_mix_kernel(in_ref, blend_ref, both_ref):
    nd, members = in_ref.shape[0], in_ref.shape[1]
    cols = in_ref.shape[3]
    blend = blend_ref[...]
    for d in range(nd):
        for b in range(members):
            place = slice((d * members + b) * cols, (d * members + b + 1) * cols)
            w = in_ref[d, b].astype(f32)
            m = blend[:, place]
            both_ref[0, :, place] = (w * m).astype(bf16)
            both_ref[1, :, place] = (w * (1.0 - m)).astype(bf16)


def place_mix(raw, blends):
    nd, nz, members, n, fine, cols = raw.shape
    width = nd * members * cols
    return pl.pallas_call(
        place_mix_kernel,
        grid=(n, nz),
        in_specs=[
            pl.BlockSpec((nd, None, members, None, fine, cols), lambda i, z: (0, z, 0, i, 0, 0)),
            pl.BlockSpec((None, 1, width), lambda i, z: (i, 0, 0)),
        ],
        out_specs=pl.BlockSpec((2, None, fine, width), lambda i, z: (0, i, z, 0)),
        out_shape=sds((2, n, nz * fine, width), bf16),
        compiler_params=params,
        cost_estimate=lasts(11),
        name="place_mix",
    )(raw, blends)


def place_emission_kernel(in_ref, out_ref):
    cols = in_ref.shape[3]
    for b in range(in_ref.shape[0]):
        out_ref[:, :, b * cols : (b + 1) * cols] = in_ref[b]


def place_emission(raw):
    nb, nz, nc, members, fine, cols = raw.shape
    out = pl.pallas_call(
        place_emission_kernel,
        grid=(nc, nz),
        in_specs=[
            pl.BlockSpec((nb, None, None, members, fine, cols), lambda c, z: (0, z, c, 0, 0, 0))
        ],
        out_specs=pl.BlockSpec((None, members, fine, nb * cols), lambda c, z: (c, 0, z, 0)),
        out_shape=sds((nc, members, nz * fine, nb * cols), bf16),
        compiler_params=params,
        cost_estimate=lasts(9),
        name="place_emission",
    )(raw)
    return out.reshape(nc * members * nz * fine, nb * cols)


def place_accept_kernel(in_ref, out_ref):
    cols = in_ref.shape[2]
    for h in range(in_ref.shape[0]):
        out_ref[:, h * cols : (h + 1) * cols] = in_ref[h]


def place_accept(raw):
    nb, nh, rows, cols = raw.shape
    return pl.pallas_call(
        place_accept_kernel,
        grid=(nb,),
        in_specs=[pl.BlockSpec((None, nh, rows, cols), lambda b: (b, 0, 0, 0))],
        out_specs=pl.BlockSpec((rows, nh * cols), lambda b: (b, 0)),
        out_shape=sds((nb * rows, nh * cols), bf16),
        compiler_params=params,
        cost_estimate=lasts(7),
        name="place_accept",
    )(raw)


def place_kernel(in_ref, out_ref):
    nd, members = in_ref.shape[0], in_ref.shape[1]
    cols = in_ref.shape[3]
    for d in range(nd):
        for b in range(members):
            place = slice((d * members + b) * cols, (d * members + b + 1) * cols)
            out_ref[:, place] = in_ref[d, b]


def place_rows(raw):
    nd, nz, members, n, fine, cols = raw.shape
    width = nd * members * cols
    return pl.pallas_call(
        place_kernel,
        grid=(n, nz),
        in_specs=[
            pl.BlockSpec((nd, None, members, None, fine, cols), lambda i, z: (0, z, 0, i, 0, 0))
        ],
        out_specs=pl.BlockSpec((None, fine, width), lambda i, z: (i, z, 0)),
        out_shape=sds((n, nz * fine, width), bf16),
        compiler_params=params,
        cost_estimate=lasts(5),
        name="place_rows",
    )(raw)


def swap(value, axis):
    return lax.ppermute(value, axis, [(0, 1), (1, 0)])


def send_far(value, team, distance):
    if distance == 1:
        return swap(value, team[-1])
    if distance == 2:
        return swap(value, team[0])
    return lax.ppermute(value, team, [(i, 3 - i) for i in range(4)])


def team_size(team):
    return 2 ** len(team)


def reorder(values, team):
    far = lax.axis_index(team[-1]) == 1
    if len(team) == 1:
        return jnp.where(far, jnp.stack([values[1], values[0]]), values)
    flipped = jnp.stack([values[1], values[0], values[3], values[2]])
    values = jnp.where(far, flipped, values)
    far = lax.axis_index(team[0]) == 1
    flipped = jnp.stack([values[2], values[3], values[0], values[1]])
    return jnp.where(far, flipped, values)


def team_exchange(values, team):
    return [values[0]] + [send_far(values[i], team, i) for i in range(1, team_size(team))]


def abs_exchange(values, team):
    by_distance = reorder(values, team)
    return reorder(jnp.stack(team_exchange(by_distance, team)), team)


def team_copies(value, team):
    if len(team) == 1:
        return [value, swap(value, team[0])]
    near = swap(value, team[1])
    side = swap(value, team[0])
    half = value.shape[0] // 2
    if half == 0:
        return [value, near, side, swap(near, team[0])]
    corner = jnp.concatenate([swap(near[:half], team[0]), swap(side[half:], team[1])], 0)
    return [value, near, side, corner]


def after(value, *events):
    return lax.optimization_barrier((value, events))[0]


def tie_kernel(*refs):
    pass


def tie(value, *events):
    anywhere = pl.BlockSpec(memory_space=pl.ANY)
    return pl.pallas_call(
        tie_kernel,
        in_specs=[anywhere] * (1 + len(events)),
        out_specs=anywhere,
        out_shape=sds(value.shape, value.dtype),
        input_output_aliases={0: 0},
        name="tie",
    )(value, *events)


def gather_tokens(value, team, event=None):
    pieces = team_copies(value, team)
    if event is not None:
        pieces[1:-1] = [after(piece, event) for piece in pieces[1:-1]]
    return [jnp.concatenate([piece, swap(piece, "c")], 0) for piece in pieces]


def core_reduce(part):
    tokens = part.shape[0] // 2
    return part[:tokens].astype(f32) + swap(part[tokens:], "c").astype(f32)


def reduce_tokens(make_part, team, early=None, late=None, hold=None, finish=None):
    def free(value):
        return value

    extra = None
    if len(team) == 1:
        away = core_reduce(make_part(1, free)).astype(bf16)

        def pin(value):
            return after(value, away)

        got = swap(away, team[0])
        work = early or late
        own = core_reduce(make_part(0, pin))
        if work:
            extra = work(pin)
            own = after(own, extra)
        return own + got.astype(f32), extra
    corner = core_reduce(make_part(3, free)).astype(bf16)
    half = corner.shape[0] // 2
    to_near = swap(corner[:half], team[0])
    to_side = swap(corner[half:], team[1])
    if early:
        extra = early(lambda v: after(v, corner))
        near, side = make_part(1, lambda v: after(v, extra)), make_part(2, lambda v: after(v, extra))
    else:
        near, side = make_part(1, free), make_part(2, free)
    if hold is not None:
        near, side = tie(near, hold), tie(side, hold)
    near, side = core_reduce(near), core_reduce(side)
    near = jnp.concatenate([near[:half] + to_near.astype(f32), near[half:]], 0).astype(bf16)
    side = jnp.concatenate([side[:half], side[half:] + to_side.astype(f32)], 0).astype(bf16)

    def pin(value):
        return after(value, near, side)

    from_near = swap(near, team[1])
    from_side = swap(side, team[0])
    own = core_reduce(make_part(0, pin))
    if late:
        extra = late(pin)
        own = after(own, extra)
    if finish is not None:
        own = tie(own, finish)
    return own + from_near.astype(f32) + from_side.astype(f32), extra


def split_rows(shards, team):
    n, rows, cols = shards.shape
    members = team_size(team)
    blocks = shards.reshape(n, members, rows // members, cols).transpose(1, 0, 2, 3)
    return abs_exchange(blocks, team)


def along_z(mine, spread):
    whole = lax.all_gather(mine, spread, axis=0, tiled=False)
    return whole.reshape((-1, lax.axis_size("z")) + mine.shape)


def scatter_weights(grads, spread):
    nd, nz, members, n, fine, cols = grads.shape
    blocks = grads.reshape(nd * nz, members, n, fine, cols)
    return lax.psum_scatter(blocks, spread, scatter_dimension=0, tiled=False)


def join_rows(mine, team):
    members, n, fine, cols = mine.shape
    mine = abs_exchange(mine, team)
    return mine.transpose(1, 0, 2, 3).reshape(n, members * fine, cols)


def z_ring(value):
    nz = lax.axis_size("z")
    got = [value] + [
        lax.ppermute(value, "z", [((i + s) % nz, i) for i in range(nz)]) for s in range(1, nz)
    ]
    twice = jnp.stack(got + got)
    start = (nz - lax.axis_index("z")) % nz
    return lax.dynamic_slice_in_dim(twice, start, nz, 0)


def sum_everywhere(value, team):
    for axis in ("c",) + team[::-1]:
        value = value + swap(value, axis)
    nz = lax.axis_size("z")
    step = 1
    while step < nz:
        value = value + lax.ppermute(value, "z", [(i, i ^ step) for i in range(nz)])
        step *= 2
    return lax.psum(value, "d") if lax.axis_size("d") > 1 else value


def layer_norm(payload_lines, gain, bias):
    center = payload_lines - jnp.mean(payload_lines, -1, keepdims=True)
    inv_scale = lax.rsqrt(jnp.mean(center * center, -1, keepdims=True) + ln_eps)
    normed = center * inv_scale
    return (normed * gain + bias, normed, inv_scale)


def norm_back(upstream_deriv, normed, inv_scale, gain):
    scaled = upstream_deriv * gain
    return inv_scale * (
        scaled
        - jnp.mean(scaled, -1, keepdims=True)
        - normed * jnp.mean(scaled * normed, -1, keepdims=True)
    )


def token_mix(current, earlier, weight):
    return (
        current.astype(f32) * weight + earlier.astype(f32) * (1.0 - weight)
    ).astype(bf16)


def on_device(
    team,
    layer_source,
    piecewise_opening_memory,
    upstream_adjoint,
    earlier_layernorm_scale,
    earlier_layernorm_shift,
    accept_blend,
    lookup_blend,
    payload_blend,
    valve_blend,
    accept_weights,
    lookup_weights,
    payload_weights,
    valve_weights,
    forgetting_loglog,
    diagonal_boost,
    groupwise_scale,
    groupwise_shift,
    emission_weights,
    later_layernorm_scale,
    later_layernorm_shift,
    feedforward_lookup_blend,
    feedforward_accept_blend,
    feedforward_lookup_weights,
    feedforward_payload_weights,
    feedforward_accept_weights,
):
    members = team_size(team)
    every = ("d",) + team + ("z", "c")
    spread = ("d", "z") if lax.axis_size("d") > 1 else "z"
    nz = lax.axis_size("z")
    nd = lax.axis_size("d")
    zi = lax.axis_index("z")
    ci = lax.axis_index("c")
    member = lax.axis_index(team)
    tokens, width = layer_source.shape
    heads_here = nz
    length = 2 * tokens
    line = [(i * 2 + j) for i in range(nz) for j in range(2)]
    down = [(i, i + 1) for i in line[:-1]]
    up = [(i + 1, i) for i in line[:-1]]

    core = ci[None].astype(jnp.int32)

    mix_shards = jnp.stack(
        [w.T for w in (accept_weights, lookup_weights, payload_weights, valve_weights)]
    )
    mix_mine = split_rows(mix_shards, team)
    residual = layer_source.astype(f32)
    normed1, hat1, inv1 = layer_norm(residual, earlier_layernorm_scale, earlier_layernorm_shift)
    local_x1 = normed1.astype(bf16)
    mix_mine, local_x1 = lax.optimization_barrier((mix_mine, local_x1))
    mix_raw = along_z(mix_mine, spread)
    tail = lax.ppermute(layer_source[-1:], "z", [(i, i + 1) for i in range(nz - 1)])
    tail = jnp.where(ci == 1, tail, swap(tail, "c"))
    halo = layer_norm(tail.astype(f32), earlier_layernorm_scale, earlier_layernorm_shift)[0]
    halo = jnp.where(zi > 0, halo, 0.0).astype(bf16)
    halos = jnp.stack([jnp.pad(h, ((0, 7), (0, 0))) for h in team_copies(halo, team)])
    whole_x1 = jnp.stack(gather_tokens(local_x1, team))
    whole_x1 = whole_x1.reshape(members, 2, tokens, width)

    vectors = jnp.stack(
        [
            forgetting_loglog,
            diagonal_boost,
            groupwise_scale.reshape(members, ATTN_WIDTH),
            groupwise_shift.reshape(members, ATTN_WIDTH),
        ]
    )
    vectors = lax.dynamic_index_in_dim(vectors, member, 1, keepdims=False)
    cols = heads_here * ATTN_WIDTH
    vectors = z_ring(vectors).transpose(1, 0, 2).reshape(4, 1, cols)
    rate, boost, gn_gain, gn_bias = jnp.exp(vectors[0]), vectors[1], vectors[2], vectors[3]
    opening = reorder(piecewise_opening_memory[0], team)
    opening = z_ring(jnp.stack(team_exchange(opening, team)))
    opening = opening.transpose(1, 3, 0, 2).reshape(members, ATTN_WIDTH, cols)

    nb_cols = emission_weights.shape[1]
    cr_rows, cr_cols = feedforward_accept_weights.shape
    lookup_raw = along_z(split_rows(feedforward_lookup_weights.T[None], team), spread)
    payload_raw = along_z(split_rows(feedforward_payload_weights[None], team), spread)
    o_raw = lax.all_gather(emission_weights, every, axis=0, tiled=False)
    cr_raw = lax.all_gather(feedforward_accept_weights, every, axis=0, tiled=False)
    whole_o = place_emission(
        o_raw.reshape(nd * members, nz, 2, members, ATTN_WIDTH, nb_cols)
    )
    lookup_t = place_rows(lookup_raw)[0]
    payload_w = place_rows(payload_raw)[0]
    whole_cr = place_accept(cr_raw.reshape(nd * members, nz * 2, cr_rows, cr_cols))

    blends = jnp.stack([accept_blend, lookup_blend, payload_blend, valve_blend])
    both_w = place_mix(mix_raw, blends[:, None, :])
    rkv, gate_pre = project(core, whole_x1, halos, both_w)
    plain_w = place_rows(mix_raw)

    run_ids = jnp.arange(nz)

    def fade(steps):
        return jnp.where(
            steps >= 0, jnp.exp(-rate * (length * jnp.maximum(steps, 0)).astype(f32)), 0.0
        )

    added = local_state(rate, rkv)
    added = z_ring(added.astype(bf16)).astype(f32)
    weight = fade((zi - 1 - run_ids)[:, None])[:, None, None, :]
    s0 = fade(zi[None, None]) * opening + jnp.sum(weight * added, 0)
    z, y, begin = mix_forward(rate, boost, gn_gain, gn_bias, s0, rkv, gate_pre)

    got = jnp.stack(team_exchange([z[i] for i in range(members)], team))
    got = reorder(got, team).reshape(members, 2, tokens, cols)
    mine = lax.dynamic_index_in_dim(got, ci, 1, keepdims=False)
    other = swap(lax.dynamic_index_in_dim(got, 1 - ci, 1, keepdims=False), "c")
    pair = jnp.where(ci == 0, jnp.stack([mine, other]), jnp.stack([other, mine]))
    z_rows = pair.transpose(2, 0, 1, 3).reshape(tokens, width)
    middle = residual + nn(after(z_rows, payload_raw), whole_o)

    normed2, hat2, inv2 = layer_norm(middle, later_layernorm_scale, later_layernorm_shift)
    local_x2 = normed2.astype(bf16)
    edge2 = lax.ppermute(local_x2[-1:], ("z", "c"), down)
    prev2 = jnp.concatenate([edge2, local_x2[:-1]], 0)
    mixed_ck = token_mix(local_x2, prev2, feedforward_lookup_blend)
    mixed_cr = token_mix(local_x2, prev2, feedforward_accept_blend)
    seq_ck = gather_tokens(mixed_ck, team)
    key_pre = [nt(piece, lookup_t) for piece in seq_ck[:-1]]
    key_pre.append(nt(after(seq_ck[-1], key_pre), lookup_t))
    key_relu = [jax.nn.relu(piece) for piece in key_pre]
    key_sq = [jnp.square(piece).astype(bf16) for piece in key_relu]
    key_relu = [piece.astype(bf16) for piece in key_relu]
    value_sum, recept2 = reduce_tokens(
        lambda i, pin: nn(pin(key_sq[i]), payload_w).astype(bf16),
        team,
        late=lambda pin: nn(pin(mixed_cr), whole_cr),
    )
    sig_two = jax.nn.sigmoid(recept2)
    block_out = (middle + sig_two * value_sum).astype(bf16)

    cot = upstream_adjoint.astype(f32)
    grad_value = (cot * sig_two).astype(bf16)
    grad_r2 = (cot * value_sum * sig_two * (1.0 - sig_two)).astype(bf16)
    seq_gv = gather_tokens(grad_value, team)
    grad_key = []
    for piece, kept in zip(seq_gv, key_relu):
        if len(grad_key) == members - 1:
            piece = tie(after(piece, grad_key), plain_w)
        grad_key.append((nt(piece, payload_w) * (2.0 * kept.astype(f32))).astype(bf16))

    def channel_weights(pin):
        first = outer_grads([pin(key_sq[0])] + key_sq[1:], seq_gv, nd, members, nz)
        second = outer_grads([pin(grad_key[0])] + grad_key[1:], seq_ck, nd, members, nz)
        return first, second

    grad_ck, (cv_part, ck_part) = reduce_tokens(
        lambda i, pin: nn(pin(grad_key[i]), lookup_t).astype(bf16), team, late=channel_weights
    )
    grad_cr = lax.optimization_barrier(nt(grad_r2, whole_cr))
    cv_sum = scatter_weights(cv_part, spread)
    ck_sum = scatter_weights(after(ck_part, cv_sum), spread)
    spread_two = local_x2.astype(f32) - prev2.astype(f32)
    chan_mix_k_part = jnp.sum(grad_ck * spread_two, 0)
    chan_mix_r_part = jnp.sum(grad_cr * spread_two, 0)
    delayed_two = grad_ck * (1.0 - feedforward_lookup_blend) + grad_cr * (
        1.0 - feedforward_accept_blend
    )
    edge_up = lax.ppermute(delayed_two[:1], ("z", "c"), up)
    grad_x2 = (
        grad_ck * feedforward_lookup_blend
        + grad_cr * feedforward_accept_blend
        + jnp.concatenate([delayed_two[1:], edge_up], 0)
    )
    ln2_gain_part = jnp.sum(grad_x2 * hat2, 0)
    ln2_bias_part = jnp.sum(grad_x2, 0)
    grad_middle = cot + norm_back(grad_x2, hat2, inv2, later_layernorm_scale)
    grad_mix = grad_middle.astype(bf16)

    grad_z = nt(grad_mix, whole_o).astype(bf16)
    grad_z = grad_z.reshape(tokens, 2, members, cols).transpose(1, 2, 0, 3)
    mine = lax.dynamic_index_in_dim(grad_z, ci, 0, keepdims=False)
    other = swap(lax.dynamic_index_in_dim(grad_z, 1 - ci, 0, keepdims=False), "c")
    pair = jnp.where(ci == 0, jnp.stack([mine, other], 1), jnp.stack([other, mine], 1))
    pair = reorder(pair.reshape(members, length, cols), team)
    grad_z = jnp.stack(team_exchange(pair, team))

    grad_gate, grad_y, added, gn_sums = gate_back(
        rate, gn_gain, gn_bias, grad_z, y, gate_pre, rkv
    )
    added = z_ring(added.astype(bf16)).astype(f32)
    weight = fade((run_ids - zi - 1)[:, None])[:, None, None, :]
    end = jnp.sum(weight * added, 0)
    dr, dk, dv, mix_sums = mix_backward(
        rate, boost, end, begin, rkv, grad_y
    )
    first = jnp.sum(fade(run_ids[:, None])[:, None, None, :] * added, 0)
    first = lax.dynamic_slice_in_dim(first, zi * ATTN_WIDTH, ATTN_WIDTH, 2)
    first = reorder(jnp.stack(team_exchange(first, team)), team)
    initial_state_gradient = first.transpose(0, 2, 1)[None]

    def edges_of(parts):
        edges = jnp.stack([g[:, 0] for g in parts], 1)
        edges = lax.ppermute(edges, "z", [(i + 1, i) for i in range(nz - 1)])
        return jnp.pad(edges[:, :, None], ((0, 0), (0, 0), (0, 7), (0, 0)))

    gate_edges = edges_of((grad_gate,))
    gate_part, gate_mix = mix_weight_grads(
        core, (grad_gate,), gate_edges, whole_x1, plain_w[3:], blends[3:], nd, members, nz
    )
    gate_sum = scatter_weights(gate_part, spread)
    main_edges = edges_of((dr, dk, dv))
    edges = tie(jnp.concatenate([main_edges, gate_edges], 1), cv_sum)

    def main_weights(pin):
        return mix_weight_grads(
            core, (pin(dr), dk, dv), main_edges, whole_x1, plain_w[:3], blends[:3], nd, members, nz
        )

    grad_x1, (main_part, main_mix) = reduce_tokens(
        lambda i, pin: project_back(
            core, i, (pin(after(dr, ck_sum)), dk, dv, grad_gate), edges, both_w
        ).reshape(length, width),
        team,
        early=main_weights,
    )
    where = jnp.stack([ci, member]).astype(jnp.int32)
    side_parts = side_grads(
        where, tie(z_rows, grad_y), grad_mix, grad_r2, mixed_cr, nd, members, nz
    )
    sides = reduce_tokens(
        lambda i, pin: pin(side_parts)[i], team, hold=dr, finish=main_part
    )[0].astype(bf16)
    sides = sides.reshape(width // 2, 2, nd, nb_cols)
    o_sum = sides[:, 0].reshape(members, nz, ATTN_WIDTH, nd, nb_cols)
    o_sum = o_sum.transpose(3, 1, 0, 2, 4).reshape(nd * nz, members * ATTN_WIDTH, nb_cols)
    cr_sum = sides[:, 1].reshape(nz, cr_cols, nd, nb_cols)
    cr_sum = cr_sum.transpose(2, 0, 1, 3).reshape(nd * nz, cr_cols, nb_cols)
    sides = jnp.concatenate([o_sum, cr_sum], 1)
    sides = lax.psum_scatter(
        sides, spread, scatter_dimension=0, tiled=False
    ).reshape(2, cr_cols, nb_cols)
    weight_o_grad = sides[0].astype(f32)
    chan_recept_grad = sides[1].T.astype(f32)

    weight_r_grad, weight_k_grad, weight_v_grad = (
        w.T.astype(f32)
        for w in join_rows(
            scatter_weights(tie(main_part, ck_sum, gate_sum), spread), team
        )
    )
    chan_value_grad = join_rows(cv_sum, team)[0].astype(f32)
    chan_key_grad = join_rows(ck_sum, team)[0].T.astype(f32)
    weight_g_grad = join_rows(gate_sum, team)[0].T.astype(f32)
    mix_parts = jnp.concatenate([main_mix[:, 0], gate_mix[:, 0]], 0)
    ln1_gain_part = jnp.sum(grad_x1 * hat1, 0)
    ln1_bias_part = jnp.sum(grad_x1, 0)
    in_grad = grad_middle + norm_back(grad_x1, hat1, inv1, earlier_layernorm_scale)

    by_head = jnp.stack(
        [
            jnp.sum(gn_sums[:, :, 0], 0),
            jnp.sum(gn_sums[:, :, 1], 0),
            jnp.sum(mix_sums[:, :, 0], 0),
            jnp.sum(mix_sums[:, :, 1], 0),
        ]
    ).reshape(4, nz, 1, 1, ATTN_WIDTH)
    placed = lax.dynamic_update_slice(
        jnp.zeros((4, nz, 2, members, ATTN_WIDTH), f32), by_head, (0, 0, ci, member, 0)
    ).reshape(4, width)
    early = jnp.concatenate(
        [
            placed,
            jnp.stack([ln2_gain_part, ln2_bias_part, chan_mix_k_part, chan_mix_r_part]),
        ],
        0,
    )
    early = sum_everywhere(early, team)
    late = jnp.concatenate([mix_parts, jnp.stack([ln1_gain_part, ln1_bias_part])], 0)
    late = sum_everywhere(late, team)
    here = lax.dynamic_slice_in_dim(
        early[:4].reshape(4, nz * 2, members * ATTN_WIDTH), zi * 2 + ci, 1, 1
    )[:, 0]
    per_head = here.reshape(4, members, ATTN_WIDTH)
    return (
        block_out,
        in_grad,
        initial_state_gradient,
        late[4],
        late[5],
        late[0],
        late[1],
        late[2],
        late[3],
        weight_r_grad,
        weight_k_grad,
        weight_v_grad,
        weight_g_grad,
        per_head[2],
        per_head[3],
        here[0],
        here[1],
        weight_o_grad,
        early[4],
        early[5],
        early[6],
        early[7],
        chan_key_grad,
        chan_value_grad,
        chan_recept_grad,
    )


def solution(mesh):
    nb, nh = mesh.shape["batch"], mesh.shape["head"]

    def whole(*args):
        attn_count = args[13].shape[0]
        members = attn_count // nh
        team = ("t1", "t0") if members == 4 else ("t0",)
        fine = Mesh(
            mesh.devices.reshape((nb // members,) + (2,) * len(team) + (nh // 2, 2)),
            ("d",) + team + ("z", "c"),
        )
        batch = ("d",) + team
        head = ("z", "c")
        tok = P(batch + head, None)
        state = P(batch, head, None, None)
        cols = P(batch, head)
        rows = P(head, batch)
        per_head = P(head, None)
        channel = P(head)
        same = P()
        in_specs = (
            (tok, state, tok)
            + (same,) * 6
            + (cols,) * 4
            + (per_head,) * 2
            + (channel,) * 2
            + (rows,)
            + (same,) * 4
            + (cols, rows, cols)
        )
        out_specs = (
            (tok, tok, state)
            + (same,) * 6
            + (cols,) * 4
            + (per_head,) * 2
            + (channel,) * 2
            + (rows,)
            + (same,) * 4
            + (cols, rows, cols)
        )
        return jax.shard_map(
            functools.partial(on_device, team),
            mesh=fine,
            in_specs=in_specs,
            out_specs=out_specs,
            check_vma=False,
        )(*args)

    return whole
```

```python
import functools

import jax
import jax.numpy as jnp
from jax import lax
from jax.experimental import pallas as pl
from jax.experimental.pallas import tpu as pltpu
from jax.sharding import Mesh
from jax.sharding import PartitionSpec as P

ATTN_WIDTH = 64
QUAD = 256

ln_eps = 1e-05
gn_eps = 0.00064
f32 = jnp.float32
bf16 = jnp.bfloat16


def nn(left, right):
    return jnp.dot(left, right, preferred_element_type=f32)


def nt(left, right):
    return lax.dot_general(left, right, (((1,), (1,)), ((), ())), preferred_element_type=f32)


def tn(left, right):
    return lax.dot_general(left, right, (((0,), (0,)), ((), ())), preferred_element_type=f32)


def head_masks():
    lane_head = lax.broadcasted_iota(jnp.int32, (1, QUAD), 1) // ATTN_WIDTH
    return [lane_head == h for h in range(QUAD // ATTN_WIDTH)]


def block_mask():
    row_head = lax.broadcasted_iota(jnp.int32, (QUAD, QUAD), 0) // ATTN_WIDTH
    col_head = lax.broadcasted_iota(jnp.int32, (QUAD, QUAD), 1) // ATTN_WIDTH
    return row_head == col_head


def only(mask, lines):
    return jnp.where(mask, lines, jnp.zeros_like(lines))


def compress(square, masks):
    return sum(
        jnp.where(m, square[h * ATTN_WIDTH : (h + 1) * ATTN_WIDTH, :], 0.0)
        for h, m in enumerate(masks)
    )


def expand(packed, blocks):
    return jnp.where(blocks, jnp.concatenate([packed] * (QUAD // ATTN_WIDTH), 0), 0.0)


def head_sum(lines, ones):
    return nn(lines.astype(bf16), ones)


def head_sum_fine(lines, ones):
    coarse = lines.astype(bf16)
    return nn(coarse, ones) + nn((lines - coarse.astype(f32)).astype(bf16), ones)


def local_state_kernel(rate_ref, k_ref, v_ref, out_ref):
    length = k_ref.shape[1]
    rate = rate_ref[...]
    remaining = (length - 1) - lax.broadcasted_iota(jnp.int32, (length, 1), 0)
    faded = (k_ref[0].astype(f32) * jnp.exp(-rate * remaining.astype(f32))).astype(bf16)
    out_ref[0] = compress(tn(v_ref[0], faded), head_masks())


def group_norm_parts(y, ones):
    center = y - head_sum_fine(y, ones) * (1.0 / ATTN_WIDTH)
    inv = lax.rsqrt(head_sum(center * center, ones) * (1.0 / ATTN_WIDTH) + gn_eps)
    return center * inv, inv


def forward_kernel(
    rate_ref, boost_ref, gain_ref, bias_ref, s0_ref, r_ref, k_ref, v_ref, g_ref,
    z_ref, y_ref, begin_ref, state,
):
    span = r_ref.shape[1]
    masks = head_masks()
    blocks = block_mask()
    ones = jnp.where(blocks, 1.0, 0.0).astype(bf16)

    @pl.when(pl.program_id(2) == 0)
    def _():
        state[...] = expand(s0_ref[0], blocks)

    rate = rate_ref[...]
    pos = lax.broadcasted_iota(jnp.int32, (span, 1), 0).astype(f32)
    r = r_ref[0].astype(f32)
    k = k_ref[0].astype(f32)
    v = v_ref[0]
    qt = (r * jnp.exp(-rate * pos)).astype(bf16)
    kt = (k * jnp.exp(rate * (pos + 1.0))).astype(bf16)
    begin = state[...]
    begin_ref[0, 0] = compress(begin, masks)
    y = nt(qt, begin.astype(bf16))
    causal = lax.broadcasted_iota(jnp.int32, (span, span), 0) > lax.broadcasted_iota(
        jnp.int32, (span, span), 1
    )
    for m in masks:
        scores = jnp.where(causal, nt(only(m, qt), kt), 0.0).astype(bf16)
        y = y + nn(scores, only(m, v))
    y = y + head_sum(r * boost_ref[...] * k, ones) * v.astype(f32)
    state[...] = jnp.exp(-rate * span) * (begin + jnp.where(blocks, tn(v, kt), 0.0))
    y_ref[0] = y
    normed, _ = group_norm_parts(y, ones)
    g = g_ref[0]
    z_ref[0] = ((normed * gain_ref[...] + bias_ref[...]) * (g * jax.nn.sigmoid(g))).astype(bf16)


def gate_back_kernel(
    rate_ref, gain_ref, bias_ref, gz_ref, y_ref, g_ref, r_ref,
    gg_ref, gy_ref, end_ref, sums_ref, total,
):
    span = r_ref.shape[1]
    step = pl.program_id(2)
    blocks = block_mask()
    ones = jnp.where(blocks, 1.0, 0.0).astype(bf16)

    @pl.when(step == 0)
    def _():
        total[...] = jnp.zeros_like(total)
        sums_ref[...] = jnp.zeros_like(sums_ref)

    normed, inv = group_norm_parts(y_ref[0], ones)
    gain = gain_ref[...]
    g = g_ref[0]
    gz = gz_ref[0].astype(f32)
    sig = jax.nn.sigmoid(g)
    grad_grouped = gz * (g * sig)
    grouped = normed * gain + bias_ref[...]
    gg_ref[0] = (gz * grouped * sig * (1.0 + g * (1.0 - sig))).astype(bf16)
    sums_ref[0, 0, 0:1, :] += jnp.sum(grad_grouped * normed, 0, keepdims=True)
    sums_ref[0, 0, 1:2, :] += jnp.sum(grad_grouped, 0, keepdims=True)
    e = grad_grouped * gain
    gy = inv * (
        e
        - head_sum_fine(e, ones) * (1.0 / ATTN_WIDTH)
        - normed * (head_sum(e * normed, ones) * (1.0 / ATTN_WIDTH))
    )
    gy = gy.astype(bf16)
    gy_ref[0] = gy
    pos = (lax.broadcasted_iota(jnp.int32, (span, 1), 0) + step * span).astype(f32)
    faded = (r_ref[0].astype(f32) * jnp.exp(-rate_ref[...] * pos)).astype(bf16)
    total[...] += tn(gy, faded)
    end_ref[0] = compress(total[...], head_masks())


def backward_kernel(
    rate_ref, boost_ref, end_ref, begin_ref, r_ref, k_ref, v_ref, gy_ref,
    dr_ref, dk_ref, dv_ref, sums_ref, carry,
):
    span = r_ref.shape[1]
    masks = head_masks()
    blocks = block_mask()
    ones = jnp.where(blocks, 1.0, 0.0).astype(bf16)

    @pl.when(pl.program_id(2) == 0)
    def _():
        carry[...] = expand(end_ref[0], blocks)
        sums_ref[...] = jnp.zeros_like(sums_ref)

    rate = rate_ref[...]
    boost = boost_ref[...]
    pos = lax.broadcasted_iota(jnp.int32, (span, 1), 0).astype(f32)
    toward = jnp.exp(-rate * pos)
    away = jnp.exp(rate * (pos + 1.0))
    r = r_ref[0].astype(f32)
    k = k_ref[0].astype(f32)
    v = v_ref[0]
    gy = gy_ref[0]
    qt = (r * toward).astype(bf16)
    kt = (k * away).astype(bf16)
    passed = jnp.exp(-rate * span) * carry[...]
    passed_low = passed.astype(bf16)
    begin = expand(begin_ref[0, 0], blocks)
    rows = lax.broadcasted_iota(jnp.int32, (span, span), 0)
    cols = lax.broadcasted_iota(jnp.int32, (span, span), 1)
    dq = nn(gy, begin.astype(bf16))
    dk = nn(v, passed_low)
    dv = nt(kt, passed_low)
    for m in masks:
        v_h, gy_h, k_h, q_h = only(m, v), only(m, gy), only(m, kt), only(m, qt)
        pairs = jnp.where(rows > cols, nt(gy_h, v), 0.0).astype(bf16)
        dq = dq + nn(pairs, k_h)
        pairs_t = jnp.where(rows < cols, nt(v_h, gy), 0.0).astype(bf16)
        dk = dk + nn(pairs_t, q_h)
        scores_t = jnp.where(rows < cols, nt(k_h, qt), 0.0).astype(bf16)
        dv = dv + nn(scores_t, gy_h)
    vf = v.astype(f32)
    gyf = gy.astype(f32)
    inner = head_sum(gyf * vf, ones)
    dv = dv + head_sum(r * boost * k, ones) * gyf
    dr_ref[0] = (dq * toward + inner * boost * k).astype(bf16)
    dk_ref[0] = (dk * away + inner * boost * r).astype(bf16)
    dv_ref[0] = dv.astype(bf16)
    held = begin.astype(bf16).astype(f32) + jnp.where(blocks, tn(v, kt), 0.0)
    decay = (
        jnp.sum(pos * dq * qt.astype(f32), 0, keepdims=True)
        - jnp.sum((pos + 1.0) * dk * kt.astype(f32), 0, keepdims=True)
        + span * jnp.sum(passed_low.astype(f32) * held, 0, keepdims=True)
    )
    sums_ref[0, 0, 0:1, :] += decay * (-rate)
    sums_ref[0, 0, 1:2, :] += jnp.sum(inner * r * k, 0, keepdims=True)
    carry[...] = passed + jnp.where(blocks, tn(gy, qt), 0.0)


VMEM_LIMIT = 56 * 1024 * 1024
params = pltpu.CompilerParams(vmem_limit_bytes=VMEM_LIMIT)


def lasts(microseconds):
    return pl.CostEstimate(
        flops=int(FLOPS_PER_US * microseconds), bytes_accessed=0, transcendentals=0
    )


FLOPS_PER_US = 3e9


def vec_spec():
    return pl.BlockSpec((1, QUAD), lambda s, q, c: (0, q))


def state_spec():
    return pl.BlockSpec((1, ATTN_WIDTH, QUAD), lambda s, q, c: (s, 0, q))


def sums_spec():
    return pl.BlockSpec((1, 1, 2, QUAD), lambda s, q, c: (s, q, 0, 0))


def sds(shape, dtype):
    return jax.ShapeDtypeStruct(shape, dtype)


def local_state(rate, rkv):
    _, segs, length, width = rkv.shape

    def block(i):
        return pl.BlockSpec((None, 1, length, QUAD), lambda s, q: (i, s, 0, q))

    return pl.pallas_call(
        local_state_kernel,
        grid=(segs, width // QUAD),
        in_specs=[pl.BlockSpec((1, QUAD), lambda s, q: (0, q)), block(1), block(2)],
        out_specs=pl.BlockSpec((1, ATTN_WIDTH, QUAD), lambda s, q: (s, 0, q)),
        out_shape=sds((segs, ATTN_WIDTH, width), f32),
        compiler_params=params,
        cost_estimate=lasts(5),
        name="local_state",
    )(rate, rkv, rkv)


def mix_forward(rate, boost, gain, bias, s0, rkv, g):
    _, segs, length, width = rkv.shape
    span = min(QUAD, length)
    count = length // span
    quads = width // QUAD
    block = pl.BlockSpec((1, span, QUAD), lambda s, q, c: (s, c, q))

    def part(i):
        return pl.BlockSpec((None, 1, span, QUAD), lambda s, q, c: (i, s, c, q))

    return pl.pallas_call(
        forward_kernel,
        grid=(segs, quads, count),
        in_specs=[vec_spec()] * 4
        + [state_spec(), part(0), part(1), part(2), block],
        out_specs=[
            block,
            block,
            pl.BlockSpec((1, 1, ATTN_WIDTH, QUAD), lambda s, q, c: (s, c, 0, q)),
        ],
        out_shape=[
            sds((segs, length, width), bf16),
            sds((segs, length, width), f32),
            sds((segs, count, ATTN_WIDTH, width), f32),
        ],
        scratch_shapes=[pltpu.VMEM((QUAD, QUAD), f32)],
        compiler_params=params,
        cost_estimate=lasts(20),
        name="mix_forward",
    )(rate, boost, gain, bias, s0, rkv, rkv, rkv, g)


def gate_back(rate, gain, bias, gz, y, g, rkv):
    _, segs, length, width = rkv.shape
    span = min(QUAD, length)
    quads = width // QUAD
    block = pl.BlockSpec((1, span, QUAD), lambda s, q, c: (s, c, q))
    lead = pl.BlockSpec((None, 1, span, QUAD), lambda s, q, c: (0, s, c, q))
    return pl.pallas_call(
        gate_back_kernel,
        grid=(segs, quads, length // span),
        in_specs=[vec_spec()] * 3 + [block, block, block, lead],
        out_specs=[block, block, state_spec(), sums_spec()],
        out_shape=[
            sds((segs, length, width), bf16),
            sds((segs, length, width), bf16),
            sds((segs, ATTN_WIDTH, width), f32),
            sds((segs, quads, 2, QUAD), f32),
        ],
        scratch_shapes=[pltpu.VMEM((QUAD, QUAD), f32)],
        compiler_params=params,
        cost_estimate=lasts(18 / 8),
        name="gate_back",
    )(rate, gain, bias, gz, y, g, rkv)


def mix_backward(rate, boost, end, begin, rkv, gy):
    _, segs, length, width = rkv.shape
    span = min(QUAD, length)
    count = length // span
    quads = width // QUAD
    block = pl.BlockSpec((1, span, QUAD), lambda s, q, c: (s, count - 1 - c, q))

    def part(i):
        return pl.BlockSpec((None, 1, span, QUAD), lambda s, q, c: (i, s, count - 1 - c, q))

    return pl.pallas_call(
        backward_kernel,
        grid=(segs, quads, count),
        in_specs=[vec_spec()] * 2
        + [
            state_spec(),
            pl.BlockSpec((1, 1, ATTN_WIDTH, QUAD), lambda s, q, c: (s, count - 1 - c, 0, q)),
        ]
        + [part(0), part(1), part(2), block],
        out_specs=[block, block, block, sums_spec()],
        out_shape=[sds((segs, length, width), bf16)] * 3 + [sds((segs, quads, 2, QUAD), f32)],
        scratch_shapes=[pltpu.VMEM((QUAD, QUAD), f32)],
        compiler_params=params,
        cost_estimate=lasts(29 / 8),
        name="mix_backward",
    )(rate, boost, end, begin, rkv, rkv, rkv, gy)


def project_kernel(core_ref, x_ref, halo_ref, w_ref, rkv_ref, gate_ref, carry):
    x = x_ref[...]
    now_w = w_ref[0].reshape(-1, x.shape[1])
    past_w = w_ref[1].reshape(-1, x.shape[1])
    now = nt(x, now_w)
    past = nt(x, past_w)

    @pl.when(pl.program_id(1) == 0)
    def _():
        carry[...] = nt(halo_ref[...], past_w)

    rows = lax.broadcasted_iota(jnp.int32, past.shape, 0)
    out = now + jnp.where(rows == 0, carry[0:1, :], pltpu.roll(past, 1, 0))
    cols = gate_ref.shape[1]
    for i in range(3):
        rkv_ref[i] = out[:, i * cols : (i + 1) * cols].astype(bf16)
    gate_ref[...] = out[:, 3 * cols :]
    carry[0:1, :] = past[past.shape[0] - 1 :, :]


def project(core, x, halos, weights):
    segs, _, tokens, width = x.shape
    cols = weights.shape[2]
    spec = pltpu.PrefetchScalarGridSpec(
        num_scalar_prefetch=1,
        grid=(segs, 2),
        in_specs=[
            pl.BlockSpec((None, None, tokens, width), lambda s, h, core: (s, h ^ core[0], 0, 0)),
            pl.BlockSpec((None, 8, width), lambda s, h, core: (s, 0, 0)),
            pl.BlockSpec((2, 4, cols, width), lambda s, h, core: (0, 0, 0, 0)),
        ],
        out_specs=[
            pl.BlockSpec((3, None, tokens, cols), lambda s, h, core: (0, s, h, 0)),
            pl.BlockSpec((None, tokens, cols), lambda s, h, core: (s, h, 0)),
        ],
        scratch_shapes=[pltpu.VMEM((8, 4 * cols), f32)],
    )
    return pl.pallas_call(
        project_kernel,
        grid_spec=spec,
        out_shape=[
            sds((3, segs, 2 * tokens, cols), bf16),
            sds((segs, 2 * tokens, cols), f32),
        ],
        compiler_params=params,
        cost_estimate=lasts(50),
        name="project",
    )(core, x, halos, weights)


def project_back_kernel(core_ref, r_ref, k_ref, v_ref, g_ref, edge_ref, w_ref, out_ref, carry):
    refs = (r_ref, k_ref, v_ref, g_ref)
    tokens = r_ref.shape[0]
    now = jnp.concatenate([ref[...] for ref in refs], 1)

    @pl.when(pl.program_id(0) == 0)
    def _():
        carry[...] = jnp.concatenate([edge_ref[i] for i in range(4)], 1).astype(f32)

    wide = now.astype(f32)
    rows = lax.broadcasted_iota(jnp.int32, wide.shape, 0)
    later = jnp.where(rows == tokens - 1, carry[0:1, :], pltpu.roll(wide, tokens - 1, 0))
    carry[0:1, :] = wide[0:1, :]
    both = jnp.concatenate([now, later.astype(bf16)], 1)
    out_ref[...] = nn(both, w_ref[...]).astype(bf16)


def project_back(core, seg, grads, edges, weights):
    segs, length, cols = grads[0].shape
    tokens = length // 2
    width = weights.shape[3]
    block = pl.BlockSpec((None, tokens, cols), lambda h, core: (seg, 1 - h, 0))
    spec = pltpu.PrefetchScalarGridSpec(
        num_scalar_prefetch=1,
        grid=(2,),
        in_specs=[block] * 4
        + [
            pl.BlockSpec((None, 4, 8, cols), lambda h, core: (seg, 0, 0, 0)),
            pl.BlockSpec((8 * cols, width), lambda h, core: (0, 0)),
        ],
        out_specs=pl.BlockSpec((None, tokens, width), lambda h, core: ((1 - h) ^ core[0], 0, 0)),
        scratch_shapes=[pltpu.VMEM((8, 4 * cols), f32)],
    )
    return pl.pallas_call(
        project_back_kernel,
        grid_spec=spec,
        out_shape=sds((2, tokens, width), bf16),
        compiler_params=params,
        cost_estimate=lasts(14 / 8),
        name="project_back",
    )(core, *grads, edges, weights.reshape(8 * cols, width))


def mix_weight_kernel(count, core_ref, *refs):
    grads, (edge_ref, x_ref, w_ref, blend_ref) = refs[:count], refs[count : count + 4]
    out_ref, mix_ref, flat, total = refs[count + 4 :]
    group, tile = pl.program_id(0), pl.program_id(1)
    segs, length, cols = grads[0].shape
    tokens = length // 2

    @pl.when(tile == 0)
    def _():
        for s in range(segs):
            for i, ref in enumerate(grads):
                here = ref[s].astype(f32)
                rows = lax.broadcasted_iota(jnp.int32, here.shape, 0)
                later = jnp.where(
                    rows == length - 1,
                    edge_ref[s, i, 0:1, :].astype(f32),
                    pltpu.roll(here, length - 1, 0),
                )
                for h in range(2):
                    at = pl.multiple_of((2 * s + (h ^ core_ref[0])) * tokens, tokens)
                    part = slice(h * tokens, (h + 1) * tokens)
                    flat[i * cols : (i + 1) * cols, pl.ds(at, tokens)] = here[part].T.astype(bf16)
                    flat[(count + i) * cols : (count + i + 1) * cols, pl.ds(at, tokens)] = (
                        later[part].T.astype(bf16)
                    )

    got = nn(flat[...], x_ref[...].reshape(segs * length, x_ref.shape[3]))
    final = group == pl.num_programs(0) - 1

    @pl.when(jnp.logical_and(group == 0, jnp.logical_not(final)))
    def _():
        total[tile] = got

    @pl.when(jnp.logical_and(group > 0, jnp.logical_not(final)))
    def _():
        total[tile] += got

    @pl.when(final)
    def _():
        whole = jnp.where(group == 0, 0.0, total[tile]) + got
        nz, fine = out_ref.shape[0], out_ref.shape[2]
        for i in range(count):
            a = whole[i * cols : (i + 1) * cols]
            b = whole[(count + i) * cols : (count + i + 1) * cols]
            blend = blend_ref[i]
            grad = (a * blend + b * (1.0 - blend)).astype(bf16)
            mix_ref[i] = jnp.sum(w_ref[i].astype(f32) * (a - b), 0, keepdims=True)
            for z in range(nz):
                out_ref[z, i] = grad[z * fine : (z + 1) * fine]


def mix_weight_grads(core, grads, edges, x, plain, blends, nd, members, nz):
    count = len(grads)
    segs, length, cols = grads[0].shape
    tokens = length // 2
    width = x.shape[3]
    tiles = nd * members
    tile = width // tiles
    fine = cols // nz
    groups = segs // 2
    block = pl.BlockSpec((2, length, cols), lambda t, n, core: (t, 0, 0))

    def last(t, n):
        return jnp.where(t == groups - 1, n, 0)

    spec = pltpu.PrefetchScalarGridSpec(
        num_scalar_prefetch=1,
        grid=(groups, tiles),
        in_specs=[block] * count
        + [
            pl.BlockSpec((2, count, 8, cols), lambda t, n, core: (t, 0, 0, 0)),
            pl.BlockSpec((2, 2, tokens, tile), lambda t, n, core: (t, 0, 0, n)),
            pl.BlockSpec((count, cols, tile), lambda t, n, core: (0, 0, last(t, n))),
            pl.BlockSpec((count, 1, tile), lambda t, n, core: (0, 0, last(t, n))),
        ],
        out_specs=[
            pl.BlockSpec(
                (None, nz, None, count, fine, tile),
                lambda t, n, core: (last(t, n) // members, 0, last(t, n) % members, 0, 0, 0),
            ),
            pl.BlockSpec((count, 1, tile), lambda t, n, core: (0, 0, last(t, n))),
        ],
        scratch_shapes=[
            pltpu.VMEM((2 * count * cols, 2 * length), bf16),
            pltpu.VMEM((tiles, 2 * count * cols, tile), f32),
        ],
    )
    return pl.pallas_call(
        functools.partial(mix_weight_kernel, count),
        grid_spec=spec,
        out_shape=[
            sds((nd, nz, members, count, fine, tile), bf16),
            sds((count, 1, width), f32),
        ],
        compiler_params=params,
        cost_estimate=lasts(13 * count / 8),
        name="mix_weight_grads",
    )(core, *grads, edges, x, plain, blends[:, None, :])


def outer_kernel(count, *refs):
    lefts, rights = refs[:count], refs[count : 2 * count]
    out_ref, flat, total = refs[2 * count :]
    group, tile = pl.program_id(0), pl.program_id(1)
    length = lefts[0].shape[0]
    final = group == count // 2 - 1
    for i in range(count // 2):

        @pl.when(group == i)
        def _(i=i):
            @pl.when(tile == 0)
            def _():
                flat[:, :length] = lefts[2 * i][...].T
                flat[:, length:] = lefts[2 * i + 1][...].T

            got = nn(flat[...], jnp.concatenate([rights[2 * i][...], rights[2 * i + 1][...]], 0))
            if i > 0:
                got = got + total[tile]
            if i < count // 2 - 1:
                total[tile] = got
            else:
                nz, fine = out_ref.shape[0], out_ref.shape[2]
                low = got.astype(bf16)
                for z in range(nz):
                    out_ref[z, 0] = low[z * fine : (z + 1) * fine, :]


def outer_grads(lefts, rights, nd, members, nz):
    length, rows = lefts[0].shape
    width = rights[0].shape[1]
    tiles = nd * members
    tile = width // tiles
    fine = rows // nz
    count = len(lefts)
    groups = count // 2

    def right(i):
        def index(t, n):
            return 0, jnp.where(t < i // 2, 0, jnp.where(t > i // 2, tiles - 1, n))

        return pl.BlockSpec((length, tile), index)

    def last(t, n):
        return jnp.where(t == groups - 1, n, 0)

    return pl.pallas_call(
        functools.partial(outer_kernel, count),
        grid=(groups, tiles),
        in_specs=[pl.BlockSpec((length, rows), lambda t, n: (0, 0))] * count
        + [right(i) for i in range(count)],
        out_specs=pl.BlockSpec(
            (None, nz, None, 1, fine, tile),
            lambda t, n: (last(t, n) // members, 0, last(t, n) % members, 0, 0, 0),
        ),
        out_shape=sds((nd, nz, members, 1, fine, tile), bf16),
        scratch_shapes=[
            pltpu.VMEM((rows, 2 * length), bf16),
            pltpu.VMEM((tiles, rows, tile), f32),
        ],
        compiler_params=params,
        cost_estimate=lasts(25 / 8),
        name="outer_grads",
    )(*lefts, *rights)


def side_kernel(nd, nz, where_ref, z_ref, gm_ref, gr_ref, cr_ref, out_ref, z_flat, gr_flat):
    distance = pl.program_id(0)
    members = pl.num_programs(0)
    core, member = where_ref[0], where_ref[1]
    width = z_ref.shape[1]
    cols = width // (nd * members)
    half = width // 2
    head = half // nz

    @pl.when(distance == 0)
    def _():
        z_flat[...] = z_ref[...].T
        for c in range(2):
            for z in range(nz):
                at = (2 * z + c) * head
                gr_flat[c * half + z * head : c * half + (z + 1) * head, :] = (
                    gr_ref[:, at : at + head].T
                )

    for d in range(nd):
        at = pl.multiple_of((d * members + (member ^ distance)) * cols, cols)
        for i, (flat, right) in enumerate(((z_flat, gm_ref), (gr_flat, cr_ref))):
            got = nn(flat[...], right[:, pl.ds(at, cols)]).astype(bf16)
            place = slice(i * nd * cols + d * cols, i * nd * cols + (d + 1) * cols)
            for c in range(2):
                out_ref[c ^ core, :, place] = got[c * half : (c + 1) * half]


def side_grads(where, z_rows, grad_mix, grad_r2, mixed_cr, nd, members, nz):
    tokens, width = z_rows.shape
    wide = width // members
    whole = pl.BlockSpec((tokens, width), lambda i, where: (0, 0))
    out = pl.pallas_call(
        functools.partial(side_kernel, nd, nz),
        grid_spec=pltpu.PrefetchScalarGridSpec(
            num_scalar_prefetch=1,
            grid=(members,),
            in_specs=[whole] * 4,
            out_specs=pl.BlockSpec(
                (None, 2, width // 2, 2 * wide), lambda i, where: (i, 0, 0, 0)
            ),
            scratch_shapes=[pltpu.VMEM((width, tokens), bf16)] * 2,
        ),
        out_shape=sds((members, 2, width // 2, 2 * wide), bf16),
        compiler_params=params,
        cost_estimate=lasts(17 / 8),
        name="side_grads",
    )(where, z_rows, grad_mix, grad_r2, mixed_cr)
    return out.reshape(members, width, 2 * wide)


def place_mix_kernel(in_ref, blend_ref, both_ref):
    nd, members = in_ref.shape[0], in_ref.shape[1]
    cols = in_ref.shape[3]
    blend = blend_ref[...]
    for d in range(nd):
        for b in range(members):
            place = slice((d * members + b) * cols, (d * members + b + 1) * cols)
            w = in_ref[d, b].astype(f32)
            m = blend[:, place]
            both_ref[0, :, place] = (w * m).astype(bf16)
            both_ref[1, :, place] = (w * (1.0 - m)).astype(bf16)


def place_mix(raw, blends):
    nd, nz, members, n, fine, cols = raw.shape
    width = nd * members * cols
    return pl.pallas_call(
        place_mix_kernel,
        grid=(n, nz),
        in_specs=[
            pl.BlockSpec((nd, None, members, None, fine, cols), lambda i, z: (0, z, 0, i, 0, 0)),
            pl.BlockSpec((None, 1, width), lambda i, z: (i, 0, 0)),
        ],
        out_specs=pl.BlockSpec((2, None, fine, width), lambda i, z: (0, i, z, 0)),
        out_shape=sds((2, n, nz * fine, width), bf16),
        compiler_params=params,
        cost_estimate=lasts(11),
        name="place_mix",
    )(raw, blends)


def place_emission_kernel(in_ref, out_ref):
    cols = in_ref.shape[3]
    for b in range(in_ref.shape[0]):
        out_ref[:, :, b * cols : (b + 1) * cols] = in_ref[b]


def place_emission(raw):
    nb, nz, nc, members, fine, cols = raw.shape
    out = pl.pallas_call(
        place_emission_kernel,
        grid=(nc, nz),
        in_specs=[
            pl.BlockSpec((nb, None, None, members, fine, cols), lambda c, z: (0, z, c, 0, 0, 0))
        ],
        out_specs=pl.BlockSpec((None, members, fine, nb * cols), lambda c, z: (c, 0, z, 0)),
        out_shape=sds((nc, members, nz * fine, nb * cols), bf16),
        compiler_params=params,
        cost_estimate=lasts(9),
        name="place_emission",
    )(raw)
    return out.reshape(nc * members * nz * fine, nb * cols)


def place_accept_kernel(in_ref, out_ref):
    cols = in_ref.shape[2]
    for h in range(in_ref.shape[0]):
        out_ref[:, h * cols : (h + 1) * cols] = in_ref[h]


def place_accept(raw):
    nb, nh, rows, cols = raw.shape
    return pl.pallas_call(
        place_accept_kernel,
        grid=(nb,),
        in_specs=[pl.BlockSpec((None, nh, rows, cols), lambda b: (b, 0, 0, 0))],
        out_specs=pl.BlockSpec((rows, nh * cols), lambda b: (b, 0)),
        out_shape=sds((nb * rows, nh * cols), bf16),
        compiler_params=params,
        cost_estimate=lasts(7),
        name="place_accept",
    )(raw)


def place_kernel(in_ref, out_ref):
    nd, members = in_ref.shape[0], in_ref.shape[1]
    cols = in_ref.shape[3]
    for d in range(nd):
        for b in range(members):
            place = slice((d * members + b) * cols, (d * members + b + 1) * cols)
            out_ref[:, place] = in_ref[d, b]


def place_rows(raw):
    nd, nz, members, n, fine, cols = raw.shape
    width = nd * members * cols
    return pl.pallas_call(
        place_kernel,
        grid=(n, nz),
        in_specs=[
            pl.BlockSpec((nd, None, members, None, fine, cols), lambda i, z: (0, z, 0, i, 0, 0))
        ],
        out_specs=pl.BlockSpec((None, fine, width), lambda i, z: (i, z, 0)),
        out_shape=sds((n, nz * fine, width), bf16),
        compiler_params=params,
        cost_estimate=lasts(5),
        name="place_rows",
    )(raw)


def swap(value, axis):
    return lax.ppermute(value, axis, [(0, 1), (1, 0)])


def send_far(value, team, distance):
    if distance == 1:
        return swap(value, team[-1])
    if distance == 2:
        return swap(value, team[0])
    return lax.ppermute(value, team, [(i, 3 - i) for i in range(4)])


def team_size(team):
    return 2 ** len(team)


def reorder(values, team):
    far = lax.axis_index(team[-1]) == 1
    if len(team) == 1:
        return jnp.where(far, jnp.stack([values[1], values[0]]), values)
    flipped = jnp.stack([values[1], values[0], values[3], values[2]])
    values = jnp.where(far, flipped, values)
    far = lax.axis_index(team[0]) == 1
    flipped = jnp.stack([values[2], values[3], values[0], values[1]])
    return jnp.where(far, flipped, values)


def team_exchange(values, team):
    return [values[0]] + [send_far(values[i], team, i) for i in range(1, team_size(team))]


def abs_exchange(values, team):
    by_distance = reorder(values, team)
    return reorder(jnp.stack(team_exchange(by_distance, team)), team)


def team_copies(value, team):
    if len(team) == 1:
        return [value, swap(value, team[0])]
    near = swap(value, team[1])
    side = swap(value, team[0])
    half = value.shape[0] // 2
    if half == 0:
        return [value, near, side, swap(near, team[0])]
    corner = jnp.concatenate([swap(near[:half], team[0]), swap(side[half:], team[1])], 0)
    return [value, near, side, corner]


def after(value, *events):
    return lax.optimization_barrier((value, events))[0]


def tie_kernel(*refs):
    pass


def tie(value, *events):
    anywhere = pl.BlockSpec(memory_space=pl.ANY)
    return pl.pallas_call(
        tie_kernel,
        in_specs=[anywhere] * (1 + len(events)),
        out_specs=anywhere,
        out_shape=sds(value.shape, value.dtype),
        input_output_aliases={0: 0},
        name="tie",
    )(value, *events)


def gather_tokens(value, team, event=None):
    pieces = team_copies(value, team)
    if event is not None:
        pieces[1:-1] = [after(piece, event) for piece in pieces[1:-1]]
    return [jnp.concatenate([piece, swap(piece, "c")], 0) for piece in pieces]


def core_reduce(part):
    tokens = part.shape[0] // 2
    return part[:tokens].astype(f32) + swap(part[tokens:], "c").astype(f32)


def reduce_tokens(make_part, team, late=None):
    def free(value):
        return value

    extra = None
    if len(team) == 1:
        away = core_reduce(make_part(1, free)).astype(bf16)

        def pin(value):
            return after(value, away)

        got = swap(away, team[0])
        work = late
        own = core_reduce(make_part(0, pin))
        if work:
            extra = work(pin)
            own = after(own, extra)
        return own + got.astype(f32), extra
    corner = core_reduce(make_part(3, free)).astype(bf16)
    half = corner.shape[0] // 2
    to_near = swap(corner[:half], team[0])
    to_side = swap(corner[half:], team[1])
    near, side = core_reduce(make_part(1, free)), core_reduce(make_part(2, free))
    near = jnp.concatenate([near[:half] + to_near.astype(f32), near[half:]], 0).astype(bf16)
    side = jnp.concatenate([side[:half], side[half:] + to_side.astype(f32)], 0).astype(bf16)

    def pin(value):
        return after(value, near, side)

    from_near = swap(near, team[1])
    from_side = swap(side, team[0])
    own = core_reduce(make_part(0, pin))
    if late:
        extra = late(pin)
        own = after(own, extra)
    return own + from_near.astype(f32) + from_side.astype(f32), extra


def reduce_first(part, team):
    sent = core_reduce(part).astype(bf16)
    if len(team) == 1:
        return sent, (swap(sent, team[0]),)
    half = sent.shape[0] // 2
    return sent, (swap(sent[:half], team[0]), swap(sent[half:], team[1]))


def reduce_second(got, near, side, team):
    half = near.shape[0] // 4
    near, side = core_reduce(near), core_reduce(side)
    near = jnp.concatenate([near[:half] + got[0].astype(f32), near[half:]], 0).astype(bf16)
    side = jnp.concatenate([side[:half], side[half:] + got[1].astype(f32)], 0).astype(bf16)
    return (near, side), (swap(near, team[1]), swap(side, team[0]))


def reduce_last(own, got):
    own = core_reduce(own)
    for piece in got:
        own = own + piece.astype(f32)
    return own


def split_rows(shards, team):
    n, rows, cols = shards.shape
    members = team_size(team)
    blocks = shards.reshape(n, members, rows // members, cols).transpose(1, 0, 2, 3)
    return abs_exchange(blocks, team)


def along_z(mine, spread):
    whole = lax.all_gather(mine, spread, axis=0, tiled=False)
    return whole.reshape((-1, lax.axis_size("z")) + mine.shape)


def scatter_weights(grads, spread):
    nd, nz, members, n, fine, cols = grads.shape
    blocks = grads.reshape(nd * nz, members, n, fine, cols)
    return lax.psum_scatter(blocks, spread, scatter_dimension=0, tiled=False)


def join_rows(mine, team):
    members, n, fine, cols = mine.shape
    mine = abs_exchange(mine, team)
    return mine.transpose(1, 0, 2, 3).reshape(n, members * fine, cols)


def z_ring(value):
    nz = lax.axis_size("z")
    got = [value] + [
        lax.ppermute(value, "z", [((i + s) % nz, i) for i in range(nz)]) for s in range(1, nz)
    ]
    twice = jnp.stack(got + got)
    start = (nz - lax.axis_index("z")) % nz
    return lax.dynamic_slice_in_dim(twice, start, nz, 0)


def sum_everywhere(value, team):
    for axis in ("c",) + team[::-1]:
        value = value + swap(value, axis)
    nz = lax.axis_size("z")
    step = 1
    while step < nz:
        value = value + lax.ppermute(value, "z", [(i, i ^ step) for i in range(nz)])
        step *= 2
    return lax.psum(value, "d") if lax.axis_size("d") > 1 else value


def layer_norm(payload_lines, gain, bias):
    center = payload_lines - jnp.mean(payload_lines, -1, keepdims=True)
    inv_scale = lax.rsqrt(jnp.mean(center * center, -1, keepdims=True) + ln_eps)
    normed = center * inv_scale
    return (normed * gain + bias, normed, inv_scale)


def norm_back(upstream_deriv, normed, inv_scale, gain):
    scaled = upstream_deriv * gain
    return inv_scale * (
        scaled
        - jnp.mean(scaled, -1, keepdims=True)
        - normed * jnp.mean(scaled * normed, -1, keepdims=True)
    )


def token_mix(current, earlier, weight):
    return (
        current.astype(f32) * weight + earlier.astype(f32) * (1.0 - weight)
    ).astype(bf16)


def on_device(
    team,
    layer_source,
    piecewise_opening_memory,
    upstream_adjoint,
    earlier_layernorm_scale,
    earlier_layernorm_shift,
    accept_blend,
    lookup_blend,
    payload_blend,
    valve_blend,
    accept_weights,
    lookup_weights,
    payload_weights,
    valve_weights,
    forgetting_loglog,
    diagonal_boost,
    groupwise_scale,
    groupwise_shift,
    emission_weights,
    later_layernorm_scale,
    later_layernorm_shift,
    feedforward_lookup_blend,
    feedforward_accept_blend,
    feedforward_lookup_weights,
    feedforward_payload_weights,
    feedforward_accept_weights,
):
    members = team_size(team)
    every = ("d",) + team + ("z", "c")
    spread = ("d", "z") if lax.axis_size("d") > 1 else "z"
    nz = lax.axis_size("z")
    nd = lax.axis_size("d")
    zi = lax.axis_index("z")
    ci = lax.axis_index("c")
    member = lax.axis_index(team)
    tokens, width = layer_source.shape
    heads_here = nz
    length = 2 * tokens
    line = [(i * 2 + j) for i in range(nz) for j in range(2)]
    down = [(i, i + 1) for i in line[:-1]]
    up = [(i + 1, i) for i in line[:-1]]

    core = ci[None].astype(jnp.int32)

    mix_shards = jnp.stack(
        [w.T for w in (accept_weights, lookup_weights, payload_weights, valve_weights)]
    )
    mix_mine = split_rows(mix_shards, team)
    residual = layer_source.astype(f32)
    normed1, hat1, inv1 = layer_norm(residual, earlier_layernorm_scale, earlier_layernorm_shift)
    local_x1 = normed1.astype(bf16)
    mix_mine, local_x1 = lax.optimization_barrier((mix_mine, local_x1))
    mix_raw = along_z(mix_mine, spread)
    tail = lax.ppermute(layer_source[-1:], "z", [(i, i + 1) for i in range(nz - 1)])
    tail = jnp.where(ci == 1, tail, swap(tail, "c"))
    halo = layer_norm(tail.astype(f32), earlier_layernorm_scale, earlier_layernorm_shift)[0]
    halo = jnp.where(zi > 0, halo, 0.0).astype(bf16)
    halos = jnp.stack([jnp.pad(h, ((0, 7), (0, 0))) for h in team_copies(halo, team)])
    whole_x1 = jnp.stack(gather_tokens(local_x1, team))
    whole_x1 = whole_x1.reshape(members, 2, tokens, width)

    vectors = jnp.stack(
        [
            forgetting_loglog,
            diagonal_boost,
            groupwise_scale.reshape(members, ATTN_WIDTH),
            groupwise_shift.reshape(members, ATTN_WIDTH),
        ]
    )
    vectors = lax.dynamic_index_in_dim(vectors, member, 1, keepdims=False)
    cols = heads_here * ATTN_WIDTH
    vectors = z_ring(vectors).transpose(1, 0, 2).reshape(4, 1, cols)
    rate, boost, gn_gain, gn_bias = jnp.exp(vectors[0]), vectors[1], vectors[2], vectors[3]
    opening = reorder(piecewise_opening_memory[0], team)
    opening = z_ring(jnp.stack(team_exchange(opening, team)))
    opening = opening.transpose(1, 3, 0, 2).reshape(members, ATTN_WIDTH, cols)

    nb_cols = emission_weights.shape[1]
    cr_rows, cr_cols = feedforward_accept_weights.shape
    lookup_raw = along_z(split_rows(feedforward_lookup_weights.T[None], team), spread)
    payload_raw = along_z(split_rows(feedforward_payload_weights[None], team), spread)
    o_raw = lax.all_gather(emission_weights, every, axis=0, tiled=False)
    cr_raw = lax.all_gather(feedforward_accept_weights, every, axis=0, tiled=False)
    whole_o = place_emission(
        o_raw.reshape(nd * members, nz, 2, members, ATTN_WIDTH, nb_cols)
    )
    lookup_t = place_rows(lookup_raw)[0]
    payload_w = place_rows(payload_raw)[0]
    whole_cr = place_accept(cr_raw.reshape(nd * members, nz * 2, cr_rows, cr_cols))

    blends = jnp.stack([accept_blend, lookup_blend, payload_blend, valve_blend])
    both_w = place_mix(mix_raw, blends[:, None, :])
    rkv, gate_pre = project(core, whole_x1, halos, both_w)
    plain_w = place_rows(mix_raw)

    run_ids = jnp.arange(nz)

    def fade(steps):
        return jnp.where(
            steps >= 0, jnp.exp(-rate * (length * jnp.maximum(steps, 0)).astype(f32)), 0.0
        )

    added = local_state(rate, rkv)
    added = z_ring(added.astype(bf16)).astype(f32)
    weight = fade((zi - 1 - run_ids)[:, None])[:, None, None, :]
    s0 = fade(zi[None, None]) * opening + jnp.sum(weight * added, 0)
    z, y, begin = mix_forward(rate, boost, gn_gain, gn_bias, s0, rkv, gate_pre)

    got = jnp.stack(team_exchange([z[i] for i in range(members)], team))
    got = reorder(got, team).reshape(members, 2, tokens, cols)
    mine = lax.dynamic_index_in_dim(got, ci, 1, keepdims=False)
    other = swap(lax.dynamic_index_in_dim(got, 1 - ci, 1, keepdims=False), "c")
    pair = jnp.where(ci == 0, jnp.stack([mine, other]), jnp.stack([other, mine]))
    z_rows = pair.transpose(2, 0, 1, 3).reshape(tokens, width)
    middle = residual + nn(after(z_rows, payload_raw), whole_o)

    normed2, hat2, inv2 = layer_norm(middle, later_layernorm_scale, later_layernorm_shift)
    local_x2 = normed2.astype(bf16)
    edge2 = lax.ppermute(local_x2[-1:], ("z", "c"), down)
    prev2 = jnp.concatenate([edge2, local_x2[:-1]], 0)
    mixed_ck = token_mix(local_x2, prev2, feedforward_lookup_blend)
    mixed_cr = token_mix(local_x2, prev2, feedforward_accept_blend)
    seq_ck = gather_tokens(mixed_ck, team)
    key_pre = [nt(piece, lookup_t) for piece in seq_ck[:-1]]
    key_pre.append(nt(after(seq_ck[-1], key_pre), lookup_t))
    key_relu = [jax.nn.relu(piece) for piece in key_pre]
    key_sq = [jnp.square(piece).astype(bf16) for piece in key_relu]
    key_relu = [piece.astype(bf16) for piece in key_relu]
    value_sum, recept2 = reduce_tokens(
        lambda i, pin: nn(pin(key_sq[i]), payload_w).astype(bf16),
        team,
        late=lambda pin: nn(pin(mixed_cr), whole_cr),
    )
    sig_two = jax.nn.sigmoid(recept2)
    block_out = (middle + sig_two * value_sum).astype(bf16)

    cot = upstream_adjoint.astype(f32)
    grad_value = (cot * sig_two).astype(bf16)
    grad_r2 = (cot * value_sum * sig_two * (1.0 - sig_two)).astype(bf16)
    seq_gv = gather_tokens(grad_value, team)
    grad_key = []
    for piece, kept in zip(seq_gv, key_relu):
        if len(grad_key) == members - 1:
            piece = tie(after(piece, grad_key), plain_w)
        grad_key.append((nt(piece, payload_w) * (2.0 * kept.astype(f32))).astype(bf16))

    def channel_weights(pin):
        first = outer_grads([pin(key_sq[0])] + key_sq[1:], seq_gv, nd, members, nz)
        second = outer_grads([pin(grad_key[0])] + grad_key[1:], seq_ck, nd, members, nz)
        return first, second

    grad_ck, (cv_part, ck_part) = reduce_tokens(
        lambda i, pin: nn(pin(grad_key[i]), lookup_t).astype(bf16), team, late=channel_weights
    )
    grad_cr = lax.optimization_barrier(nt(grad_r2, whole_cr))
    cv_sum = scatter_weights(cv_part, spread)
    ck_sum = scatter_weights(after(ck_part, cv_sum), spread)
    spread_two = local_x2.astype(f32) - prev2.astype(f32)
    chan_mix_k_part = jnp.sum(grad_ck * spread_two, 0)
    chan_mix_r_part = jnp.sum(grad_cr * spread_two, 0)
    delayed_two = grad_ck * (1.0 - feedforward_lookup_blend) + grad_cr * (
        1.0 - feedforward_accept_blend
    )
    edge_up = lax.ppermute(delayed_two[:1], ("z", "c"), up)
    grad_x2 = (
        grad_ck * feedforward_lookup_blend
        + grad_cr * feedforward_accept_blend
        + jnp.concatenate([delayed_two[1:], edge_up], 0)
    )
    ln2_gain_part = jnp.sum(grad_x2 * hat2, 0)
    ln2_bias_part = jnp.sum(grad_x2, 0)
    grad_middle = cot + norm_back(grad_x2, hat2, inv2, later_layernorm_scale)
    grad_mix = grad_middle.astype(bf16)

    grad_z = nt(grad_mix, whole_o).astype(bf16)
    grad_z = grad_z.reshape(tokens, 2, members, cols).transpose(1, 2, 0, 3)
    mine = lax.dynamic_index_in_dim(grad_z, ci, 0, keepdims=False)
    other = swap(lax.dynamic_index_in_dim(grad_z, 1 - ci, 0, keepdims=False), "c")
    pair = jnp.where(ci == 0, jnp.stack([mine, other], 1), jnp.stack([other, mine], 1))
    pair = reorder(pair.reshape(members, length, cols), team)
    grad_z = jnp.stack(team_exchange(pair, team))

    grad_gate, grad_y, added, gn_sums = gate_back(
        rate, gn_gain, gn_bias, grad_z, y, gate_pre, rkv
    )
    added = z_ring(added.astype(bf16)).astype(f32)
    weight = fade((run_ids - zi - 1)[:, None])[:, None, None, :]
    end = jnp.sum(weight * added, 0)
    first = jnp.sum(fade(run_ids[:, None])[:, None, None, :] * added, 0)
    first = lax.dynamic_slice_in_dim(first, zi * ATTN_WIDTH, ATTN_WIDTH, 2)
    first = reorder(jnp.stack(team_exchange(first, team)), team)
    initial_state_gradient = first.transpose(0, 2, 1)[None]

    where = jnp.stack([ci, member]).astype(jnp.int32)
    side_parts = side_grads(
        where, tie(z_rows, grad_y), grad_mix, grad_r2, mixed_cr, nd, members, nz
    )
    side_sent, side_got = reduce_first(side_parts[members - 1], team)

    def edges_of(parts):
        edges = jnp.stack([g[:, 0] for g in parts], 1)
        edges = lax.ppermute(edges, "z", [(i + 1, i) for i in range(nz - 1)])
        return jnp.pad(edges[:, :, None], ((0, 0), (0, 0), (0, 7), (0, 0)))

    gate_edges = edges_of((grad_gate,))
    gate_part, gate_mix = mix_weight_grads(
        core, (grad_gate,), gate_edges, whole_x1, plain_w[3:], blends[3:], nd, members, nz
    )
    gate_sum = scatter_weights(gate_part, spread)
    end = tie(end, gate_part)
    dr, dk, dv, mix_sums = mix_backward(
        rate, boost, end, begin, rkv, grad_y
    )
    main_edges = edges_of((dr, dk, dv))
    edges = tie(jnp.concatenate([main_edges, gate_edges], 1), cv_sum)

    def back(i, held):
        grads = (held, dk, dv, grad_gate)
        return project_back(core, i, grads, edges, both_w).reshape(length, width)

    x1_sent, x1_got = reduce_first(back(members - 1, dr), team)
    held = tie(dr, x1_sent)
    main_part, main_mix = mix_weight_grads(
        core, (held, dk, dv), main_edges, whole_x1, plain_w[:3], blends[:3], nd, members, nz
    )
    held = tie(held, main_part)
    if members > 2:
        x1_sent, x1_got = reduce_second(x1_got, back(1, held), back(2, held), team)
        side_near, side_side = tie(side_parts[1], *x1_sent), tie(side_parts[2], *x1_sent)
        side_sent, side_got = reduce_second(side_got, side_near, side_side, team)
    held = tie(held, *jax.tree.leaves(x1_sent), *jax.tree.leaves(side_sent))
    grad_x1 = reduce_last(back(0, held), x1_got)
    main_sum = scatter_weights(tie(main_part, ck_sum, gate_sum), spread)
    mix_parts = jnp.concatenate([main_mix[:, 0], gate_mix[:, 0]], 0)

    side_own = tie(side_parts[0], grad_x1)
    sides = reduce_last(side_own, side_got).astype(bf16)
    sides = sides.reshape(width // 2, 2, nd, nb_cols)
    o_sum = sides[:, 0].reshape(members, nz, ATTN_WIDTH, nd, nb_cols)
    o_sum = o_sum.transpose(3, 1, 0, 2, 4).reshape(nd * nz, members * ATTN_WIDTH, nb_cols)
    cr_sum = sides[:, 1].reshape(nz, cr_cols, nd, nb_cols)
    cr_sum = cr_sum.transpose(2, 0, 1, 3).reshape(nd * nz, cr_cols, nb_cols)
    sides = jnp.concatenate([o_sum, cr_sum], 1)
    sides = lax.psum_scatter(sides, spread, scatter_dimension=0, tiled=False)
    sides = sides.reshape(2, cr_cols, nb_cols)
    weight_o_grad = sides[0].astype(f32)
    chan_recept_grad = sides[1].T.astype(f32)
    weight_r_grad, weight_k_grad, weight_v_grad = (
        w.T.astype(f32) for w in join_rows(main_sum, team)
    )
    chan_value_grad = join_rows(cv_sum, team)[0].astype(f32)
    chan_key_grad = join_rows(ck_sum, team)[0].T.astype(f32)
    weight_g_grad = join_rows(gate_sum, team)[0].T.astype(f32)
    ln1_gain_part = jnp.sum(grad_x1 * hat1, 0)
    ln1_bias_part = jnp.sum(grad_x1, 0)
    in_grad = grad_middle + norm_back(grad_x1, hat1, inv1, earlier_layernorm_scale)

    by_head = jnp.stack(
        [
            jnp.sum(gn_sums[:, :, 0], 0),
            jnp.sum(gn_sums[:, :, 1], 0),
            jnp.sum(mix_sums[:, :, 0], 0),
            jnp.sum(mix_sums[:, :, 1], 0),
        ]
    ).reshape(4, nz, 1, 1, ATTN_WIDTH)
    placed = lax.dynamic_update_slice(
        jnp.zeros((4, nz, 2, members, ATTN_WIDTH), f32), by_head, (0, 0, ci, member, 0)
    ).reshape(4, width)
    early = jnp.concatenate(
        [
            placed,
            jnp.stack([ln2_gain_part, ln2_bias_part, chan_mix_k_part, chan_mix_r_part]),
        ],
        0,
    )
    early = sum_everywhere(early, team)
    late = jnp.concatenate([mix_parts, jnp.stack([ln1_gain_part, ln1_bias_part])], 0)
    late = sum_everywhere(late, team)
    here = lax.dynamic_slice_in_dim(
        early[:4].reshape(4, nz * 2, members * ATTN_WIDTH), zi * 2 + ci, 1, 1
    )[:, 0]
    per_head = here.reshape(4, members, ATTN_WIDTH)
    return (
        block_out,
        in_grad,
        initial_state_gradient,
        late[4],
        late[5],
        late[0],
        late[1],
        late[2],
        late[3],
        weight_r_grad,
        weight_k_grad,
        weight_v_grad,
        weight_g_grad,
        per_head[2],
        per_head[3],
        here[0],
        here[1],
        weight_o_grad,
        early[4],
        early[5],
        early[6],
        early[7],
        chan_key_grad,
        chan_value_grad,
        chan_recept_grad,
    )


def solution(mesh):
    nb, nh = mesh.shape["batch"], mesh.shape["head"]

    def whole(*args):
        attn_count = args[13].shape[0]
        members = attn_count // nh
        team = ("t1", "t0") if members == 4 else ("t0",)
        fine = Mesh(
            mesh.devices.reshape((nb // members,) + (2,) * len(team) + (nh // 2, 2)),
            ("d",) + team + ("z", "c"),
        )
        batch = ("d",) + team
        head = ("z", "c")
        tok = P(batch + head, None)
        state = P(batch, head, None, None)
        cols = P(batch, head)
        rows = P(head, batch)
        per_head = P(head, None)
        channel = P(head)
        same = P()
        in_specs = (
            (tok, state, tok)
            + (same,) * 6
            + (cols,) * 4
            + (per_head,) * 2
            + (channel,) * 2
            + (rows,)
            + (same,) * 4
            + (cols, rows, cols)
        )
        out_specs = (
            (tok, tok, state)
            + (same,) * 6
            + (cols,) * 4
            + (per_head,) * 2
            + (channel,) * 2
            + (rows,)
            + (same,) * 4
            + (cols, rows, cols)
        )
        return jax.shard_map(
            functools.partial(on_device, team),
            mesh=fine,
            in_specs=in_specs,
            out_specs=out_specs,
            check_vma=False,
        )(*args)

    return whole
```
